128 devices in a mesh: seq: 8 (over y, core), head: 16 (over x, z).
Axes of the slice: x: 4, y: 4, z: 4, core: 2. Of those that a mesh axis runs over, the one named last changes fastest.
Arguments:
- hidden_states: bfloat16 [64, 64, 8192], P('seq', None, 'head'), may hold values from -33 to 33
- span_group: int32 [64, 1], replicated, may hold values from 0 to 7; in each aligned block of 8 rows (0 to 7, 8 to 15, ...) at most 2 rows name the same one
- span_slot: int32 [64], replicated, may hold values from 0 to 7
- span_block: int32 [64], replicated, may hold values from 0 to 127
- prompt_len: int32 [64], P('seq'), may hold values from 4096 to 8192
- new_tokens: bfloat16 [2, 64, 8192], P(None, 'seq', 'head'), may hold values from -12 to 12
- norm_gain: bfloat16 [2, 8192], replicated, may hold values from 0.25 to 1.75
- w_q: bfloat16 [8192, 4096], P(None, 'head'), may hold values from -8 to 8
- w_kv: bfloat16 [8192, 2, 4096], P(None, None, 'head'), may hold values from -0.0625 to 0.0625
- w_o: bfloat16 [4096, 8192], P('head'), may hold values from -0.09375 to 0.09375
- w_gate_up: bfloat16 [8192, 2, 16384], P(None, None, ('seq', 'head')), may hold values from -0.0625 to 0.0625
- w_down: bfloat16 [16384, 8192], P(('seq', 'head')), may hold values from -0.1875 to 0.1875
Outputs:
- mixed: bfloat16 [2, 64, 8192], P(None, 'seq', 'head')
The draws below stay inside these ranges and needn't reach their ends.
Inputs may be any that keep to these rules, and one draw needn't show every extreme that they name: `span_group`: among the 8 spans of one index of seq (rows of one device, in order), at most 2 name the same group.
All inputs are finite; a program needn't handle non-finite values.
Results may differ from the reference program's by a relative error of at most 0.015.
Values may be sent and summed in bfloat16 or wider, within the bound.
A program may use at most 128 MiB of HBM per device.

```python
import math
import jax
import jax.numpy as jnp
import numpy as np
from jax import lax

D = 8192
HEADS = 32
HD = 128
FF = 16384
RG = 8
STEPS = 2
C = 64
CD = 8
PROMPT = 8192
CAP = 2
BLOCKS = 128
SPANS = 64
NREQ = 64
N_SEQ = 8


def spread_scales(key, dims, low, high):
    return jnp.exp(jax.random.uniform(key, dims, jnp.float32, math.log(low), math.log(high)))


def feature_ramp(low, high):
    steps = jnp.arange(D).astype(jnp.float32) / (D - 1)
    return jnp.exp(math.log(low) + steps * (math.log(high) - math.log(low)))


def draw_hidden_states(key, part):
    key = jax.random.fold_in(key, 11)
    key_base, key_rows, key_cols = jax.random.split(key, 3)
    dims = (SPANS, C, D)
    entries = jnp.clip(jax.random.normal(key_base, dims, jnp.float32), -3.0, 3.0)
    ramp = feature_ramp(0.4, 2.4)
    entries = entries * spread_scales(key_rows, (SPANS, C, 1), 0.3, 3.0) * spread_scales(key_cols, (D,), 0.5, 1.5) * ramp
    return entries.astype(jnp.bfloat16)


def draw_new_tokens(key, part):
    key = jax.random.fold_in(key, 23)
    key_base, key_rows, key_cols = jax.random.split(key, 3)
    dims = (STEPS, NREQ, D)
    entries = jnp.clip(jax.random.normal(key_base, dims, jnp.float32), -3.0, 3.0)
    entries = entries * spread_scales(key_rows, (STEPS, NREQ, 1), 0.6, 1.6) * spread_scales(key_cols, (D,), 0.25, 2.5)
    return entries.astype(jnp.bfloat16)


def draw_w_q(key, part):
    key = jax.random.fold_in(key, 37)
    key_base, key_heads = jax.random.split(key, 2)
    entries = jnp.clip(jax.random.normal(key_base, (D, HEADS, HD), jnp.float32), -4.0, 4.0) * (1.0 / math.sqrt(D))
    boost = spread_scales(key_heads, (1, HEADS, 1), 0.7, 1.4)
    return jnp.clip(entries * boost, -8.0, 8.0).reshape(D, HEADS * HD).astype(jnp.bfloat16)


def plant(drawn, key, least, top_value):
    spot = [jax.random.randint(jax.random.fold_in(key, axis), (), 0, length) for axis, length in enumerate(drawn.shape)]
    main_axis = drawn.shape.index(max(drawn.shape))
    next_to = spot[:main_axis] + [(spot[main_axis] + 1) % drawn.shape[main_axis]] + spot[main_axis + 1:]
    return drawn.at[tuple(spot)].set(least).at[tuple(next_to)].set(top_value)


def strengthened(result, stream_key, source, target, blocks, factor):
    def block_of(axis_at):
        return (jnp.arange(result.shape[axis_at]) // (result.shape[axis_at] // blocks)).reshape((-1,) + (1,) * (result.ndim - 1 - axis_at))

    one_side = jax.random.permutation(stream_key, blocks)[block_of(target)]
    far = (block_of(target) + blocks // 2) % blocks
    return jnp.where((block_of(source) == one_side) | (block_of(source) == far), factor * result, result)


def level_of(own_key, shape, cuts, least, largest):
    def one(dim, shards_of):
        steps = jax.random.uniform(jax.random.fold_in(jax.random.fold_in(own_key, 6), dim), (shards_of,), jnp.float32, least / len(cuts), largest / len(cuts))
        return jnp.repeat(jnp.exp(steps), shape[dim] // shards_of).reshape((-1,) + (1,) * (len(shape) - dim - 1))

    gain = one(*cuts[0])
    for cut in cuts[1:]:
        gain = gain * one(*cut)
    return gain


def assign_block(stream_key, own, number, rows, number_of, top, reach, skew):
    ranking = jax.random.permutation(stream_key, number_of)
    packed, usual = portions_of(number_of, rows * top, reach, skew, True), portions_of(number_of, rows * top, reach, skew, False)
    places = jnp.arange(number_of)

    def named(lengths, rotation):
        used = int((lengths > 0).sum())
        fixed = max(1, used // 4)
        shifted = fixed + (places - fixed + rotation * (used - fixed)) % max(1, number_of - fixed)
        return jnp.zeros((number_of,), jnp.int32).at[ranking[jnp.where(places < fixed, places, shifted)]].set(jnp.asarray(lengths, jnp.int32))

    lengths = jnp.where(number % 4 == 0, named(packed, number // 4), named(usual, number - number // 4 - 1))
    mixed = jax.random.permutation(jax.random.fold_in(own, 3), number_of)
    donor, sink = mixed[0:number_of // 2 * 2:2], mixed[1:number_of // 2 * 2:2]
    margin = jnp.minimum(lengths[donor] - 1, reach - lengths[sink]) // 2
    margin = jnp.where((donor == ranking[0]) | (sink == ranking[0]) | (lengths[sink] == 0), 0, jnp.maximum(margin, 0))
    shifted = jax.random.randint(jax.random.fold_in(own, 4), (number_of // 2,), 0, 1 << 20) % (margin + 1)
    lengths = lengths.at[donor].add(-shifted).at[sink].add(shifted)
    labels = jnp.searchsorted(jnp.cumsum(lengths), jnp.arange(rows * top), side="right").astype(jnp.int32)
    table = labels.reshape(top, rows).T
    table = table[jax.random.permutation(jax.random.fold_in(own, 1), rows)]
    rotation = jax.random.randint(jax.random.fold_in(own, 2), (rows, 1), 0, top)
    return jnp.take_along_axis(table, (jnp.arange(top)[None, :] + rotation) % top, axis=1)


def portions_of(count, total, most, slope, full):
    weights = [(1 << 20) // math.isqrt(grade ** slope) + 1 for grade in range(1, count + 1)]
    largest = most if full else min(most, max(-(-total // count), total * weights[0] // sum(weights)))
    least = 1 if total - largest >= count - 1 else 0
    holding, spare = [largest] + [least] * (count - 1), total - largest - least * (count - 1)
    while spare > 0:
        candidates = [i for i in range(1, count) if holding[i] < largest] or [i for i in range(1, count) if holding[i] < most]
        pool, left = sum([weights[i] for i in candidates]), spare
        for i in candidates:
            more = min(most - holding[i], max(1, left * weights[i] // pool), spare)
            holding[i] = holding[i] + more
            spare = spare - more
    return np.array(holding)


def normal_values(rng, shape, spread, limit, cuts=(), kind=jnp.bfloat16):
    array = spread * jax.random.normal(rng, shape, jnp.float32)
    if cuts:
        array = array * level_of(rng, shape, cuts, -0.22, 0.18)
    return jnp.clip(array, -limit, limit).astype(kind)


def bell_draw_with(rng, shape, deviation, reach, cuts, heavy, kind=jnp.bfloat16):
    array = deviation * jax.random.normal(rng, shape, jnp.float32)
    if cuts:
        array = array * level_of(rng, shape, cuts, -0.22, 0.18)
    return jnp.clip(strengthened(array, jax.random.fold_in(rng, 3), *heavy), -reach, reach).astype(kind)


def setup_inputs(seed: int = 0) -> dict:
    key_of = jax.random.split(jax.random.key(seed), 13)
    hidden_states = draw_hidden_states(jax.random.fold_in(key_of[12], 71), 0)
    span_group_keys = jax.random.split(jax.random.fold_in(key_of[1], 1), SPANS // CD)
    span_group_turns = jax.random.permutation(jax.random.fold_in(key_of[1], 3), SPANS // CD)
    span_group = jax.vmap(lambda own, number: assign_block(jax.random.fold_in(key_of[1], 2), own, number, CD, N_SEQ, 1, CAP, 2))(span_group_keys, span_group_turns).reshape((SPANS, 1))
    span_slot = plant(jax.random.randint(key_of[2], (SPANS,), 0, RG), jax.random.fold_in(key_of[2], 1), 0, RG - 1).astype(jnp.int32)
    span_block = plant(jax.random.randint(key_of[3], (SPANS,), 0, BLOCKS), jax.random.fold_in(key_of[3], 1), 0, BLOCKS - 1).astype(jnp.int32)
    prompt_len = plant(jax.random.randint(key_of[4], (NREQ,), PROMPT // 2, PROMPT + 1), jax.random.fold_in(key_of[4], 1), PROMPT // 2, PROMPT).astype(jnp.int32)
    new_tokens = draw_new_tokens(jax.random.fold_in(key_of[12], 71), 0)
    norm_gain = jnp.clip(1.0 + 0.15 * jax.random.normal(key_of[6], (2, D), jnp.float32), 0.25, 1.75).astype(jnp.bfloat16)
    w_q = draw_w_q(jax.random.fold_in(key_of[12], 71), 0)
    w_kv = normal_values(key_of[8], (D, 2, HEADS * HD), D ** -0.5, 0.0625, ((2, 16),))
    w_o = normal_values(key_of[9], (HEADS * HD, D), (HEADS * HD) ** -0.5, 0.09375, ((0, 16),))
    w_gate_up = normal_values(key_of[10], (D, 2, FF), D ** -0.5, 0.0625, ((2, 128),))
    w_down = bell_draw_with(key_of[11], (FF, D), FF ** -0.5, 0.1875, ((0, 128),), (0, 1, 128, 5.5))
    return {"hidden_states": hidden_states, "span_group": span_group, "span_slot": span_slot, "span_block": span_block, "prompt_len": prompt_len, "new_tokens": new_tokens, "norm_gain": norm_gain, "w_q": w_q, "w_kv": w_kv, "w_o": w_o, "w_gate_up": w_gate_up, "w_down": w_down}


EPS = 1e-05
THETA = 10000.0
MASKED = -1e+30

def rope_angles(positions):
    half_dim = HD // 2
    freqs = jnp.exp(jnp.arange(half_dim).astype(jnp.float32) * (-2.0 * math.log(THETA) / HD))
    angles = positions.astype(jnp.float32)[..., None] * freqs
    return (jnp.cos(angles), jnp.sin(angles))

def rotate(vectors, cosine, sine_table):
    half_dim = HD // 2
    first_half = vectors[..., :half_dim]
    second_half = vectors[..., half_dim:]
    cosine = cosine[..., None, :]
    sine_table = sine_table[..., None, :]
    return jnp.concatenate([first_half * cosine - second_half * sine_table, first_half * sine_table + second_half * cosine], axis=-1)

def rms_normed(values, gain_row):
    mean_square = lax.optimization_barrier(jnp.mean(values * values, axis=-1))
    return (values * lax.rsqrt(mean_square + EPS)[..., None] * gain_row).astype(jnp.bfloat16)

def attend_heads(query_rows, cached_key_rows, cached_value_rows, new_keys, new_values, allowed):
    attention_score_scale = 1.0 / math.sqrt(HD)
    step_count = query_rows.shape[0]
    query_single_precision = query_rows.astype(jnp.float32)
    cached_entries = jnp.einsum('unij,oij->iuno', query_single_precision, cached_key_rows.astype(jnp.float32)) * attention_score_scale
    cached_entries = jnp.where(allowed[None, None], cached_entries, MASKED)
    fresh = jnp.einsum('srhd,urhd->hsru', query_single_precision, new_keys.astype(jnp.float32)) * attention_score_scale
    causal = jnp.arange(step_count)[None, :] <= jnp.arange(step_count)[:, None]
    fresh = jnp.where(causal[None, :, None, :], fresh, MASKED)
    top_score = jnp.maximum(lax.optimization_barrier(jnp.max(cached_entries, axis=-1)), lax.optimization_barrier(jnp.max(fresh, axis=-1)))[..., None]
    cached_exp = jnp.exp(cached_entries - top_score)
    fresh_exp = jnp.exp(fresh - top_score)
    totals = lax.optimization_barrier(jnp.sum(cached_exp, axis=-1, keepdims=True)) + lax.optimization_barrier(jnp.sum(fresh_exp, axis=-1, keepdims=True))
    cached_probability = (cached_exp / totals).astype(jnp.bfloat16)
    fresh_prob = (fresh_exp / totals).astype(jnp.bfloat16)
    summed_output = jnp.einsum('gfxv,vgw->fxgw', cached_probability.astype(jnp.float32), cached_value_rows.astype(jnp.float32))
    summed_output = summed_output + jnp.einsum('hsru,urhd->srhd', fresh_prob.astype(jnp.float32), new_values.astype(jnp.float32))
    return summed_output.astype(jnp.bfloat16)

def reference(hidden_states, span_group, span_slot, span_block, prompt_len, new_tokens, norm_gain, w_q, w_kv, w_o, w_gate_up, w_down):
    inner_width = HEADS * HD
    gains = norm_gain.astype(jnp.float32)
    span_rows = hidden_states.reshape(SPANS * C, D).astype(jnp.float32)
    kv_weights = w_kv.reshape(D, 2 * inner_width)
    span_kv = jnp.dot(rms_normed(span_rows, gains[0]), kv_weights, preferred_element_type=jnp.float32)
    offsets = jnp.arange(C, dtype=jnp.int32)
    positions = (span_block[:, None] * C + offsets[None, :]).reshape(SPANS * C)
    owners = jnp.broadcast_to((span_group[:, 0] * RG + span_slot)[:, None], (SPANS, C)).reshape(SPANS * C)
    live = positions < prompt_len[owners]
    cosine, sine_table = rope_angles(positions)
    cached_key_rows = rotate(span_kv[:, :inner_width].reshape(SPANS * C, HEADS, HD), cosine, sine_table).astype(jnp.bfloat16)
    cached_value_rows = span_kv[:, inner_width:].reshape(SPANS * C, HEADS, HD).astype(jnp.bfloat16)
    tokens = new_tokens.astype(jnp.float32)
    flat_tokens = rms_normed(tokens, gains[0]).reshape(STEPS * NREQ, D)
    token_positions = prompt_len[None, :] + jnp.arange(STEPS, dtype=jnp.int32)[:, None]
    token_cos, token_sin = rope_angles(token_positions)
    query_rows = rotate(jnp.dot(flat_tokens, w_q, preferred_element_type=jnp.float32).reshape(STEPS, NREQ, HEADS, HD), token_cos, token_sin).astype(jnp.bfloat16)
    fresh_kv = jnp.dot(flat_tokens, kv_weights, preferred_element_type=jnp.float32).reshape(STEPS, NREQ, 2, HEADS, HD)
    new_keys = rotate(fresh_kv[:, :, 0], token_cos, token_sin).astype(jnp.bfloat16)
    new_values = fresh_kv[:, :, 1].astype(jnp.bfloat16)
    allowed = (owners[None, :] == jnp.arange(NREQ, dtype=jnp.int32)[:, None]) & live[None, :]
    pieces = []
    for first_head in range(0, HEADS, 8):
        last_head = first_head + 8
        pieces.append(attend_heads(query_rows[:, :, first_head:last_head], cached_key_rows[:, first_head:last_head], cached_value_rows[:, first_head:last_head], new_keys[:, :, first_head:last_head], new_values[:, :, first_head:last_head], allowed))
    attended = jnp.concatenate(pieces, axis=2)
    attn_out = jnp.dot(attended.reshape(STEPS * NREQ, inner_width), w_o, preferred_element_type=jnp.float32).reshape(STEPS, NREQ, D)
    residual = tokens + attn_out
    ffn_input = rms_normed(residual, gains[1]).reshape(STEPS * NREQ, D)
    gate_up = jnp.dot(ffn_input, w_gate_up.reshape(D, 2 * FF), preferred_element_type=jnp.float32)
    activated = (jax.nn.silu(gate_up[:, :FF]) * gate_up[:, FF:]).astype(jnp.bfloat16)
    ffn_out = jnp.dot(activated, w_down, preferred_element_type=jnp.float32).reshape(STEPS, NREQ, D)
    return (residual + ffn_out).astype(jnp.bfloat16)
```

```python
import math

import jax
import jax.numpy as jnp
from jax import lax
from jax.experimental import pallas as pl
from jax.experimental.pallas import tpu as pltpu
from jax.sharding import PartitionSpec as P

D = 8192
HD = 128
C = 64
CD = 8
CAP = 2


EPS = 1e-05
THETA = 10000.0
MASKED = -1e30


MESH = pl.DeviceIdType.MESH
BF = jnp.bfloat16
F32 = jnp.float32


def tail_kernel(
    att_ref, tok_ref, gain_ref, wo_hbm, wgu_hbm, wd_hbm, out_ref,
    wo, wgu, wd, send_a, recv_a, rows, own_terms, send_d1, recv_d1, send_d2, recv_d2, send_d3, recv_d3, res,
    wsem, sa, ra, s1, r1, s2, r2, s3, r3, sd1, rd1, sd2, rd2, sd3, rd3,
):
    s = lax.axis_index("seq")
    h = lax.axis_index("head")
    y = s // 2
    c = lax.rem(s, 2)
    slot = c * 4 + y
    pair = s + 1 - 2 * c

    def at_head(k):
        return lax.rem(h + k, 16)

    barrier = pltpu.get_barrier_semaphore()

    @pl.loop(1, 16)
    def _(k):
        pl.semaphore_signal(barrier, inc=1, device_id=(s, at_head(k)), device_id_type=MESH)

    @pl.loop(1, 8)
    def _(k):
        pl.semaphore_signal(barrier, inc=1, device_id=(lax.rem(s + k, 8), h), device_id_type=MESH)

    def weight_copies(j):
        cols = pl.ds(pl.multiple_of(j * 512, 512), 512)
        return (
            pltpu.make_async_copy(wo_hbm.at[:, cols], wo.at[j], wsem.at[0, j]),
            pltpu.make_async_copy(wgu_hbm.at[cols], wgu.at[j], wsem.at[1, j]),
            pltpu.make_async_copy(wd_hbm.at[:, cols], wd.at[j], wsem.at[2, j]),
        )

    for which in range(3):
        @pl.loop(0, 16)
        def _(j):
            weight_copies(j)[which].start()

    pl.semaphore_wait(barrier, 22)

    def remote(src, dst, ssem, rsem, device):
        return pltpu.make_async_remote_copy(
            src_ref=src, dst_ref=dst, send_sem=ssem, recv_sem=rsem, device_id=device, device_id_type=MESH
        )

    @pl.loop(0, 16)
    def _(j):
        weight_copies(j)[0].wait()

    def copy_a(k):
        t = at_head(k)
        return remote(send_a.at[t], recv_a.at[h], sa.at[t], ra.at[h], (s, t))

    def came_a(k):
        f = at_head(16 - k)
        return remote(send_a.at[f], recv_a.at[f], sa.at[f], ra.at[f], (s, f))

    @pl.loop(1, 16)
    def _(k):
        t = at_head(k)
        send_a[t] = jnp.dot(att_ref[...], wo[t], preferred_element_type=F32).astype(BF)
        copy_a(k).start()

    res[...] = tok_ref[...].astype(F32) + jnp.dot(att_ref[...], wo[h], preferred_element_type=F32)

    @pl.loop(1, 16)
    def _(k):
        came_a(k).wait_recv()
        res[...] += recv_a[at_head(16 - k)].astype(F32)

    rows[h, slot] = res[...].astype(BF)

    def copy_1(k):
        t = lax.rem(s + k, 8)
        return remote(rows.at[h, slot], rows.at[h, slot], s1.at[t], r1.at[s], (t, h))

    def came_1(k):
        f = lax.rem(s + 8 - k, 8)
        place = lax.rem(f, 2) * 4 + f // 2
        return remote(rows.at[h, place], rows.at[h, place], s1.at[f], r1.at[f], (f, h))

    @pl.loop(1, 8)
    def _(k):
        copy_1(k).start()

    @pl.loop(1, 8)
    def _(k):
        came_1(k).wait_recv()

    mine = pl.ds(c * 4, 4)
    other = pl.ds(4 - c * 4, 4)

    def copy_2(k):
        t = at_head(k)
        return remote(rows.at[h, mine], rows.at[h, mine], s2.at[t], r2.at[h], (s, t))

    def came_2(k):
        f = at_head(16 - k)
        return remote(rows.at[f, mine], rows.at[f, mine], s2.at[f], r2.at[f], (s, f))

    def copy_3(k):
        f = at_head(16 - k)
        return remote(rows.at[f, mine], rows.at[f, mine], s3.at[f], r3.at[f], (pair, h))

    def came_3(k):
        f = at_head(16 - k)
        return remote(rows.at[f, other], rows.at[f, other], s3.at[f], r3.at[f], (pair, h))

    @pl.loop(1, 16)
    def _(k):
        copy_2(k).start()

    @pl.loop(0, 16)
    def _(j):
        weight_copies(j)[1].wait()
        weight_copies(j)[2].wait()

    def block(j, carry):
        acc, squares = carry
        part = rows[j].reshape(128, 512).astype(F32)
        sq = part * part
        squares = squares + (sq[:, 0:128] + sq[:, 128:256]) + (sq[:, 256:384] + sq[:, 384:512])
        scaled = (part * gain_ref[j]).astype(BF)
        return acc + jnp.dot(scaled, wgu[j], preferred_element_type=F32), squares

    carry = block(h, (jnp.zeros((128, 256), F32), jnp.zeros((128, 128), F32)))

    def step(k, carry):
        came_2(k).wait_recv()
        copy_3(k).start()
        came_3(k).wait_recv()
        return block(at_head(16 - k), carry)

    acc, squares = lax.fori_loop(1, 16, step, carry)
    scale = lax.rsqrt(jnp.sum(squares, axis=1, keepdims=True) / D + EPS)
    gate = acc[:, 0:128] * scale
    up = acc[:, 128:256] * scale
    act = (gate / (1.0 + jnp.exp(-gate)) * up).astype(BF)

    def copy_d1(t):
        return remote(send_d1.at[t], recv_d1.at[t], sd1.at[t], rd1.at[t], (pair, h))

    def copy_d2(t):
        return remote(send_d2.at[t], recv_d2.at[h], sd2.at[t], rd2.at[h], (s, t))

    def came_d2(f):
        return remote(send_d2.at[f], recv_d2.at[f], sd2.at[f], rd2.at[f], (s, f))

    @pl.loop(0, 16)
    def _(k):
        t = at_head(k + 1)
        terms = jnp.dot(act, wd[t], preferred_element_type=F32)
        low, high = terms[0:64], terms[64:128]
        own_terms[t] = jnp.where(c == 0, low, high)
        send_d1[t] = jnp.where(c == 0, high, low).astype(BF)
        copy_d1(t).start()

    @pl.loop(0, 15)
    def _(k):
        t = at_head(k + 1)
        copy_d1(t).wait_recv()
        send_d2[t] = (own_terms[t] + recv_d1[t].astype(F32)).astype(BF)
        copy_d2(t).start()

    copy_d1(h).wait_recv()
    own_terms[h] = own_terms[h] + recv_d1[h].astype(F32)

    @pl.loop(1, 16)
    def _(k):
        f = at_head(16 - k)
        came_d2(f).wait_recv()
        own_terms[h] += recv_d2[f].astype(F32)

    def copy_d3(k):
        t = lax.rem(y + k, 4)
        return remote(send_d3.at[t], recv_d3.at[y], sd3.at[t], rd3.at[y], (t * 2 + c, h))

    def came_d3(k):
        f = lax.rem(y + 4 - k, 4)
        return remote(send_d3.at[f], recv_d3.at[f], sd3.at[f], rd3.at[f], (f * 2 + c, h))

    send_d3[...] = own_terms[h].reshape(4, 16, 512).astype(BF)
    for k in range(1, 4):
        copy_d3(k).start()
    total = res[...] + own_terms[h, pl.ds(pl.multiple_of(y * 16, 16), 16)]
    for k in range(1, 4):
        came_d3(k).wait_recv()
        total = total + recv_d3[lax.rem(y + 4 - k, 4)].astype(F32)
    out_ref[...] = total.astype(BF)

    @pl.loop(1, 16)
    def _(k):
        copy_a(k).wait_send()
        copy_2(k).wait_send()
        copy_3(k).wait_send()
        copy_d1(at_head(k)).wait_send()
        copy_d2(at_head(k)).wait_send()

    copy_d1(h).wait_send()

    @pl.loop(1, 8)
    def _(k):
        copy_1(k).wait_send()

    for k in range(1, 4):
        copy_d3(k).wait_send()


def tail(attended, tokens, gain, w_o, w_gu, w_d):
    vmem = pl.BlockSpec(memory_space=pltpu.VMEM)
    hbm = pl.BlockSpec(memory_space=pl.ANY)
    dma = pltpu.SemaphoreType.DMA
    return pl.pallas_call(
        tail_kernel,
        name="tail",
        out_shape=jax.ShapeDtypeStruct((16, 512), BF),
        in_specs=[vmem, vmem, vmem, hbm, hbm, hbm],
        out_specs=vmem,
        scratch_shapes=[
            pltpu.VMEM((16, 256, 512), BF),
            pltpu.VMEM((16, 512, 256), BF),
            pltpu.VMEM((16, 128, 512), BF),
            pltpu.VMEM((16, 16, 512), BF),
            pltpu.VMEM((16, 16, 512), BF),
            pltpu.VMEM((16, 8, 16, 512), BF),
            pltpu.VMEM((16, 64, 512), F32),
            pltpu.VMEM((16, 64, 512), BF),
            pltpu.VMEM((16, 64, 512), BF),
            pltpu.VMEM((16, 64, 512), BF),
            pltpu.VMEM((16, 64, 512), BF),
            pltpu.VMEM((4, 16, 512), BF),
            pltpu.VMEM((4, 16, 512), BF),
            pltpu.VMEM((16, 512), F32),
            dma((3, 16)),
            dma((16,)), dma((16,)), dma((8,)), dma((8,)), dma((16,)), dma((16,)), dma((16,)), dma((16,)),
            dma((16,)), dma((16,)), dma((16,)), dma((16,)), dma((4,)), dma((4,)),
        ],
        compiler_params=pltpu.CompilerParams(
            collective_id=1, has_side_effects=True, vmem_limit_bytes=56 * 2**20
        ),
    )(attended, tokens, gain, w_o, w_gu, w_d)


def rope_angles(positions):
    half_dim = HD // 2
    freqs = jnp.exp(jnp.arange(half_dim).astype(jnp.float32) * (-2.0 * math.log(THETA) / HD))
    angles = positions.astype(jnp.float32)[..., None] * freqs
    return (jnp.cos(angles), jnp.sin(angles))


def rotate(vectors, cosine, sine_table):
    half_dim = HD // 2
    first_half = vectors[..., :half_dim]
    second_half = vectors[..., half_dim:]
    cosine = cosine[..., None, :]
    sine_table = sine_table[..., None, :]
    return jnp.concatenate(
        [
            first_half * cosine - second_half * sine_table,
            first_half * sine_table + second_half * cosine,
        ],
        axis=-1,
    )


def normalize(values, mean_square, gain_part):
    return (values * lax.rsqrt(mean_square + EPS)[..., None] * gain_part).astype(jnp.bfloat16)


def pack_slots(selected_slots, incoming_blocks):
    return jnp.einsum(
        "nju,uak->njak", selected_slots, incoming_blocks, preferred_element_type=jnp.float32
    ).astype(jnp.bfloat16)


def attend(query_rows, cached_key_rows, cached_value_rows, new_keys, new_values, allowed):
    attention_score_scale = 1.0 / math.sqrt(HD)
    step_count = query_rows.shape[0]
    cached_entries = (
        jnp.einsum(
            "unij,oij->iuno", query_rows, cached_key_rows, preferred_element_type=jnp.float32
        )
        * attention_score_scale
    )
    cached_entries = jnp.where(allowed[None, None], cached_entries, MASKED)
    fresh = (
        jnp.einsum("srhd,urhd->hsru", query_rows, new_keys, preferred_element_type=jnp.float32)
        * attention_score_scale
    )
    causal = jnp.arange(step_count)[None, :] <= jnp.arange(step_count)[:, None]
    fresh = jnp.where(causal[None, :, None, :], fresh, MASKED)
    top_score = jnp.maximum(jnp.max(cached_entries, axis=-1), jnp.max(fresh, axis=-1))[..., None]
    cached_exp = jnp.exp(cached_entries - top_score)
    fresh_exp = jnp.exp(fresh - top_score)
    totals = jnp.sum(cached_exp, axis=-1, keepdims=True) + jnp.sum(
        fresh_exp, axis=-1, keepdims=True
    )
    cached_probability = (cached_exp / totals).astype(jnp.bfloat16)
    fresh_prob = (fresh_exp / totals).astype(jnp.bfloat16)
    summed_output = jnp.einsum(
        "gfxv,vgw->fxgw", cached_probability, cached_value_rows, preferred_element_type=jnp.float32
    )
    summed_output = summed_output + jnp.einsum(
        "hsru,urhd->srhd", fresh_prob, new_values, preferred_element_type=jnp.float32
    )
    return summed_output.astype(jnp.bfloat16)


def local(
    hidden_states,
    span_group,
    span_slot,
    span_block,
    prompt_len,
    new_tokens,
    norm_gain,
    w_q,
    w_kv,
    w_o,
    w_gate_up,
    w_down,
):
    seq_count = lax.axis_size("seq")
    head_count = lax.axis_size("head")
    my_group = lax.axis_index("seq")
    my_head = lax.axis_index("head")
    part_width = D // head_count
    inner_dev = w_q.shape[1]
    heads_dev = inner_dev // HD
    step_count = new_tokens.shape[0]
    req_dev = new_tokens.shape[1]
    gain_full = norm_gain.astype(jnp.float32)
    gain_attn = lax.dynamic_slice_in_dim(gain_full[0], my_head * part_width, part_width, 0)
    kv_flat = w_kv.reshape(D, 2 * inner_dev)
    all_groups = span_group[:, 0].reshape(seq_count, CD)
    all_slots = span_slot.reshape(seq_count, CD)
    all_blocks = span_block.reshape(seq_count, CD)
    span_order = jnp.arange(CD)
    earlier = span_order[None, :] < span_order[:, None]
    same_dest = all_groups[:, :, None] == all_groups[:, None, :]
    send_ranks = jnp.sum((same_dest & earlier[None]).astype(jnp.int32), axis=2)
    dest_iota = jnp.arange(seq_count)
    slot_iota = jnp.arange(CAP)
    own_groups = lax.dynamic_index_in_dim(all_groups, my_group, 0, keepdims=False)
    own_ranks = lax.dynamic_index_in_dim(send_ranks, my_group, 0, keepdims=False)
    sending = (own_groups[None, None, :] == dest_iota[:, None, None]) & (
        own_ranks[None, None, :] == slot_iota[None, :, None]
    )
    send_pick = sending.astype(jnp.bfloat16)
    arriving = (all_groups[:, None, :] == my_group) & (
        send_ranks[:, None, :] == slot_iota[None, :, None]
    )
    occupied = jnp.any(arriving, axis=2)
    arrived_slot = jnp.sum(jnp.where(arriving, all_slots[:, None, :], 0), axis=2)
    arrived_block = jnp.sum(jnp.where(arriving, all_blocks[:, None, :], 0), axis=2)
    offsets = jnp.arange(C)
    arrived_positions = (arrived_block[:, :, None] * C + offsets).reshape(-1)
    arrived_owner = jnp.broadcast_to(arrived_slot[:, :, None], (seq_count, CAP, C)).reshape(-1)
    arrived_live = jnp.broadcast_to(occupied[:, :, None], (seq_count, CAP, C)).reshape(-1)
    packed = pack_slots(send_pick, hidden_states)
    arrived = lax.all_to_all(packed, "seq", split_axis=0, concat_axis=0, tiled=True)
    arrived_float = arrived.reshape(-1, part_width).astype(jnp.float32)
    squares = lax.psum(jnp.sum(arrived_float * arrived_float, axis=1), "head")
    normed_rows = normalize(arrived_float, squares / D, gain_attn)
    kv_sum = jnp.dot(
        lax.all_gather(normed_rows, "head", axis=1, tiled=True),
        kv_flat,
        preferred_element_type=jnp.float32,
    )
    cache_cos, cache_sin = rope_angles(arrived_positions)
    cached_key_rows = rotate(
        kv_sum[:, :inner_dev].reshape(-1, heads_dev, HD), cache_cos, cache_sin
    ).astype(jnp.bfloat16)
    cached_value_rows = kv_sum[:, inner_dev:].reshape(-1, heads_dev, HD).astype(jnp.bfloat16)
    token_full = lax.all_gather(new_tokens, "head", axis=2, tiled=True)
    token_float = token_full.astype(jnp.float32)
    normed_tokens = normalize(
        token_float, jnp.mean(token_float * token_float, axis=-1), gain_full[0]
    )
    flat_tokens = normed_tokens.reshape(-1, D)
    token_positions = prompt_len[None, :] + jnp.arange(step_count, dtype=jnp.int32)[:, None]
    token_cos, token_sin = rope_angles(token_positions)
    query_rows = rotate(
        jnp.dot(flat_tokens, w_q, preferred_element_type=jnp.float32).reshape(
            step_count, req_dev, heads_dev, HD
        ),
        token_cos,
        token_sin,
    ).astype(jnp.bfloat16)
    fresh_kv = jnp.dot(flat_tokens, kv_flat, preferred_element_type=jnp.float32).reshape(
        step_count, req_dev, 2, heads_dev, HD
    )
    new_keys = rotate(fresh_kv[:, :, 0], token_cos, token_sin).astype(jnp.bfloat16)
    new_values = fresh_kv[:, :, 1].astype(jnp.bfloat16)
    allowed = (
        (arrived_owner[None, :] == jnp.arange(req_dev)[:, None])
        & (arrived_positions[None, :] < prompt_len[:, None])
        & arrived_live[None, :]
    )
    attended = attend(query_rows, cached_key_rows, cached_value_rows, new_keys, new_values, allowed)
    out = tail(
        attended.reshape(-1, inner_dev),
        new_tokens.reshape(-1, part_width),
        gain_full[1].reshape(head_count, 1, part_width),
        w_o,
        w_gate_up.reshape(D, -1),
        w_down,
    )
    return out.reshape(step_count, req_dev, part_width)


def solution(mesh):
    placed = (
        P("seq", None, "head"),
        P(),
        P(),
        P(),
        P("seq"),
        P(None, "seq", "head"),
        P(),
        P(None, "head"),
        P(None, None, "head"),
        P("head", None),
        P(None, None, ("seq", "head")),
        P(("seq", "head"), None),
    )
    return jax.shard_map(
        local, mesh=mesh, in_specs=placed, out_specs=P(None, "seq", "head"), check_vma=False
    )
```

```python
import math

import jax
import jax.numpy as jnp
import numpy as np
from jax import lax
from jax.experimental import pallas as pl
from jax.experimental.pallas import tpu as pltpu
from jax.sharding import PartitionSpec as P

D = 8192
HD = 128
C = 64
CD = 8
EPS = 1e-05
THETA = 10000.0
MASKED = -1e30
SCALE = 1.0 / math.sqrt(HD)
MESH = pl.DeviceIdType.MESH
BF = jnp.bfloat16
F32 = jnp.float32


def fold_squares(part):
    sq = part * part
    return (sq[:, 0:128] + sq[:, 128:256]) + (sq[:, 256:384] + sq[:, 384:512])


def rotate(vectors, cosine, sine):
    return vectors * cosine + pltpu.roll(vectors, 64, 1) * sine


ORDER = (
    (-1, 0), (1, 0), (0, -1), (0, 1), (2, 0), (-1, -1), (-1, 1), (1, -1), (1, 1), (0, 2),
    (2, -1), (2, 1), (-1, 2), (1, 2), (2, 2),
)


def layer_kernel(
    x_ref, tok_ref, gain_ref, rep_kv_ref, rep_gu_ref, sel_ref, match_ref, pos_ref, cosk_ref, sink_ref, cosq_ref, sinq_ref,
    plen_ref, wq_hbm, wkv_hbm, wo_hbm, wgu_hbm, wd_hbm, out_ref,
    wq, raw, wkv, wo, wgu, wd, pick_kv, pick_gu, spans, kv_acc, span_ss, toks, queries, partials, fresh,
    send_a, recv_a, rows, own_terms, send_d1, recv_d1, send_d2, recv_d2, send_d3, recv_d3, res,
    wsem, gsem, sx, rx, st, rt, sq, rq, sp, rp,
    sa, ra, s1, r1, s2, r2, s3, r3, sd1, rd1, sd2, rd2, sd3, rd3,
):
    s = lax.axis_index("seq")
    h = lax.axis_index("head")
    y = s // 2
    c = lax.rem(s, 2)
    slot = c * 4 + y
    pair = s + 1 - 2 * c
    px = h // 4
    pz = lax.rem(h, 4)

    def at_head(k):
        return lax.rem(h + k, 16)

    def at_seq(k):
        return lax.rem(s + k, 8)

    barrier = pltpu.get_barrier_semaphore()

    @pl.loop(1, 16)
    def _(k):
        pl.semaphore_signal(barrier, inc=1, device_id=(s, at_head(k)), device_id_type=MESH)

    @pl.loop(1, 8)
    def _(k):
        pl.semaphore_signal(barrier, inc=1, device_id=(at_seq(k), h), device_id_type=MESH)

    def weight_copy(which, j):
        cols = pl.ds(pl.multiple_of(j * 512, 512), 512)
        if which == 0:
            return pltpu.make_async_copy(wkv_hbm.at[pl.ds(pl.multiple_of(j * 2048, 2048), 2048)], raw.at[j], wsem.at[0, j])
        if which == 1:
            return pltpu.make_async_copy(wq_hbm.at[cols], wq.at[j], wsem.at[1, j])
        if which == 2:
            return pltpu.make_async_copy(wo_hbm.at[:, cols], wo.at[j], wsem.at[2, j])
        return pltpu.make_async_copy(wd_hbm.at[:, cols], wd.at[j], wsem.at[3, j])

    def gate_up_copy(j):
        return pltpu.make_async_copy(
            wgu_hbm.at[pl.ds(pl.multiple_of(j * 1024, 1024), 1024)], raw.at[j, pl.ds(0, 1024)], gsem.at[j]
        )

    for which in range(4):
        @pl.loop(0, 16)
        def _(j):
            weight_copy(which, j).start()

    def remote(src, dst, ssem, rsem, device):
        return pltpu.make_async_remote_copy(
            src_ref=src, dst_ref=dst, send_sem=ssem, recv_sem=rsem, device_id=device, device_id_type=MESH
        )

    row = lax.broadcasted_iota(jnp.int32, (256, 256), 0)
    col = lax.broadcasted_iota(jnp.int32, (256, 256), 1)
    low = lax.rem(col, 4)
    pick_kv[...] = jnp.where(row == (lax.rem(low, 2) * 2 + low // 2) * 64 + col // 4, 1.0, 0.0).astype(F32)
    pick_gu[...] = jnp.where(row == lax.rem(col, 2) * 128 + col // 2, 1.0, 0.0).astype(F32)

    spans[h] = x_ref[...]
    toks[h] = tok_ref[...]
    queries[s, 16:32] = plen_ref[...]
    kv_acc[...] = jnp.zeros_like(kv_acc)
    span_ss[...] = jnp.zeros_like(span_ss)

    pl.semaphore_wait(barrier, 22)

    def copy_t(k):
        t = at_head(k)
        return remote(toks.at[h], toks.at[h], st.at[t], rt.at[h], (s, t))

    def came_t(k):
        f = at_head(16 - k)
        return remote(toks.at[f], toks.at[f], st.at[f], rt.at[f], (s, f))

    @pl.loop(1, 16)
    def _(k):
        copy_t(k).start()

    def place(half, a, b):
        dx, dz = (a, b) if half == 0 else (b, a)
        return lax.rem(px + dx + 4, 4) * 4 + lax.rem(pz + dz + 4, 4)

    sends = []

    def push(half, block, part, axis, way):
        there = place(half, way, 0) if axis == 0 else place(half, 0, way)
        first, size, sem = ((0, 128, 0), (128, 128, 1), (0, 256, 0))[part]
        where = spans.at[block, pl.ds(half * 256 + first, size)]
        copy = remote(where, where, sx.at[len(sends)], rx.at[block, half * 2 + sem], (s, there))
        copy.start()
        sends.append(copy)

    def wait_for(half, block, part):
        first, size, sem = ((0, 128, 0), (128, 128, 1), (0, 256, 0))[part]
        where = spans.at[block, pl.ds(half * 256 + first, size)]
        remote(where, where, sx.at[0], rx.at[block, half * 2 + sem], (s, h)).wait_recv()

    def unpack(block):
        weight_copy(0, block).wait()

        @pl.loop(0, 8)
        def _(b):
            pick = (pick_kv[...] * rep_kv_ref[block * 8 + b]).astype(BF)
            part = raw[block, pl.ds(pl.multiple_of(b * 256, 256), 256)]
            got = jnp.dot(pick, part, preferred_element_type=F32).astype(BF)
            at = pl.ds(pl.multiple_of(b * 64, 64), 64)
            for i in range(4):
                wkv[block, at, pl.ds(i * 128, 128)] = got[i * 64:(i + 1) * 64]

    def take(half, block):
        @pl.loop(0, 2)
        def _(i):
            at = pl.ds(pl.multiple_of(half * 256 + i * 128, 128), 128)
            part = spans[block, at]
            span_ss[at] += fold_squares(part.astype(F32))
            kv_acc[at] += jnp.dot(part, wkv[block], preferred_element_type=F32)

    for half in range(2):
        for way in (1, -1):
            push(half, h, 2, 0, way)
    for half in range(2):
        for way in (1, -1):
            push(half, h, 2, 1, way)

    unpack(h)
    for half in range(2):
        take(half, h)

    def project_queries():
        @pl.loop(0, 16)
        def _(j):
            weight_copy(1, j).wait()

        @pl.loop(1, 16)
        def _(k):
            came_t(k).wait_recv()

        def body(j, carry):
            acc, ss = carry
            part = toks[j].astype(F32)
            scaled = (part * gain_ref[j]).astype(BF)
            return acc + jnp.dot(scaled, wq[j], preferred_element_type=F32), ss + fold_squares(part)

        acc, ss = lax.fori_loop(0, 16, body, (jnp.zeros((16, 256), F32), jnp.zeros((16, 128), F32)))
        scale = lax.rsqrt(jnp.sum(ss, axis=1, keepdims=True) / D + EPS)
        for j in range(2):
            at = slice(j * 128, (j + 1) * 128)
            queries[s, 0:16, at] = rotate(acc[:, at] * scale, cosq_ref[...], sinq_ref[...]).astype(BF)

        @pl.loop(1, 8)
        def _(k):
            copy_q(k).start()

        return scale

    def copy_q(k):
        t = at_seq(k)
        return remote(queries.at[s], queries.at[s], sq.at[t], rq.at[s], (t, h))

    def came_q(k):
        f = at_seq(8 - k)
        return remote(queries.at[f], queries.at[f], sq.at[f], rq.at[f], (f, h))

    unpacked = set()
    token_scale = None
    for number, (a, b) in enumerate(ORDER):
        blocks = [place(half, a, b) for half in range(2)]
        for half in range(2):
            block = blocks[half]
            parts = (0, 1) if (a == 2 and b == 0) or b == 2 else (2,)
            for part in parts:
                wait_for(half, block, part)
            if b == 0:
                if a == -1:
                    push(half, block, 0, 0, 1)
                if a == 1:
                    push(half, block, 1, 0, -1)
                push(half, block, 2, 1, 1)
                push(half, block, 2, 1, -1)
            elif b == -1:
                push(half, block, 0, 1, 1)
            elif b == 1:
                push(half, block, 1, 1, -1)
        for half in range(2):
            source = (a % 4, b % 4) if half == 0 else (b % 4, a % 4)
            if source not in unpacked:
                unpacked.add(source)
                unpack(blocks[half])
            take(half, blocks[half])
        if number == 3:
            token_scale = project_queries()

    @pl.loop(0, 16)
    def _(j):
        gate_up_copy(j).start()

    def project_fresh(j, acc):
        return acc + jnp.dot(toks[j], wkv[j], preferred_element_type=F32)

    new_kv = lax.fori_loop(0, 16, project_fresh, jnp.zeros((16, 512), F32)) * token_scale

    @pl.loop(1, 8)
    def _(k):
        came_q(k).wait_recv()

    chosen = jnp.dot(sel_ref[...], queries[...].reshape(256, 256), preferred_element_type=F32)
    length = chosen[16:24, 0:1] * 128.0 + chosen[24:32, 0:1]
    length = jnp.concatenate([length, length], axis=0)
    token_span = lax.broadcasted_iota(jnp.int32, (16, 512), 1) // C
    row_span = lax.rem(lax.broadcasted_iota(jnp.int32, (16, 512), 0), CD)
    live = (token_span == row_span) & (pos_ref[...] < length)
    span_scale = lax.rsqrt(jnp.sum(span_ss[...], axis=1, keepdims=True) / D + EPS)
    lanes = lax.broadcasted_iota(jnp.int32, (16, 128), 1)
    for j in range(2):
        at = slice(j * 128, (j + 1) * 128)
        keys = rotate(kv_acc[:, at] * span_scale, cosk_ref[...], sink_ref[...]).astype(BF)
        values = (kv_acc[:, 256 + j * 128:384 + j * 128] * span_scale).astype(BF)
        scores = lax.dot_general(
            chosen[0:16, at].astype(BF), keys, (((1,), (1,)), ((), ())), preferred_element_type=F32
        ) * SCALE
        scores = jnp.where(live, scores, MASKED)
        top = jnp.max(scores, axis=1, keepdims=True)
        weights = jnp.where(live, jnp.exp(scores - top), 0.0)
        total = jnp.sum(weights, axis=1, keepdims=True)
        partials[s, j * 16:(j + 1) * 16, 0:128] = jnp.dot(weights.astype(BF), values, preferred_element_type=F32)
        partials[s, j * 16:(j + 1) * 16, 128:256] = jnp.where(lanes < 64, top, total)

    def copy_p(k):
        t = at_seq(k)
        return remote(partials.at[s], partials.at[s], sp.at[t], rp.at[s], (t, h))

    def came_p(k):
        f = at_seq(8 - k)
        return remote(partials.at[f], partials.at[f], sp.at[f], rp.at[f], (f, h))

    @pl.loop(1, 8)
    def _(k):
        copy_p(k).start()

    for j in range(2):
        at = slice(j * 128, (j + 1) * 128)
        fresh[j] = rotate(new_kv[:, at], cosq_ref[...], sinq_ref[...]).astype(BF).astype(F32)
        fresh[2 + j] = new_kv[:, 256 + j * 128:384 + j * 128].astype(BF).astype(F32)

    @pl.loop(0, 16)
    def _(j):
        gate_up_copy(j).wait()

        @pl.loop(0, 4)
        def _(b):
            pick = (pick_gu[...] * rep_gu_ref[j * 4 + b]).astype(BF)
            part = raw[j, pl.ds(pl.multiple_of(b * 256, 256), 256)]
            got = jnp.dot(pick, part, preferred_element_type=F32).astype(BF)
            at = pl.ds(pl.multiple_of(b * 128, 128), 128)
            wgu[j, at, 0:128] = got[0:128]
            wgu[j, at, 128:256] = got[128:256]

    @pl.loop(1, 8)
    def _(k):
        came_p(k).wait_recv()

    match = match_ref[...] > 0.0
    own_q = queries[s, 0:16].astype(F32)
    heads = []
    for j in range(2):
        steps = []
        for t in range(2):
            block = partials[:, pl.ds(j * 16 + t * 8, 8), :].reshape(64, 256)
            stats = block[:, 128:256].T
            tops, sums = stats[0:8], stats[64:72]
            q = own_q[t * 8:(t + 1) * 8, j * 128:(j + 1) * 128]
            fresh_scores = [
                jnp.sum(q * fresh[j, u * 8:(u + 1) * 8], axis=1, keepdims=True) * SCALE for u in range(t + 1)
            ]
            best = jnp.max(jnp.where(match, tops, MASKED), axis=1, keepdims=True)
            for score in fresh_scores:
                best = jnp.maximum(best, score)
            factor = jnp.where(match, jnp.exp(jnp.where(match, tops, best) - best), 0.0)
            total = jnp.sum(factor * sums, axis=1, keepdims=True)
            value = jnp.dot(factor, block[:, 0:128], precision=lax.Precision.HIGHEST, preferred_element_type=F32)
            for u, score in enumerate(fresh_scores):
                e = jnp.exp(score - best)
                total = total + e
                value = value + e * fresh[2 + j, u * 8:(u + 1) * 8]
            steps.append(value / total)
        heads.append(jnp.concatenate(steps, axis=0))
    att = jnp.concatenate(heads, axis=1).astype(BF)

    @pl.loop(0, 16)
    def _(j):
        weight_copy(2, j).wait()

    def copy_a(k):
        t = at_head(k)
        return remote(send_a.at[t], recv_a.at[h], sa.at[t], ra.at[h], (s, t))

    def came_a(k):
        f = at_head(16 - k)
        return remote(send_a.at[f], recv_a.at[f], sa.at[f], ra.at[f], (s, f))

    @pl.loop(1, 16)
    def _(k):
        t = at_head(k)
        send_a[t] = jnp.dot(att, wo[t], preferred_element_type=F32).astype(BF)
        copy_a(k).start()

    res[...] = tok_ref[...].astype(F32) + jnp.dot(att, wo[h], preferred_element_type=F32)

    @pl.loop(1, 16)
    def _(k):
        came_a(k).wait_recv()
        res[...] += recv_a[at_head(16 - k)].astype(F32)

    rows[h, slot] = res[...].astype(BF)

    def copy_1(k):
        t = lax.rem(s + k, 8)
        return remote(rows.at[h, slot], rows.at[h, slot], s1.at[t], r1.at[s], (t, h))

    def came_1(k):
        f = lax.rem(s + 8 - k, 8)
        place = lax.rem(f, 2) * 4 + f // 2
        return remote(rows.at[h, place], rows.at[h, place], s1.at[f], r1.at[f], (f, h))

    @pl.loop(1, 8)
    def _(k):
        copy_1(k).start()

    @pl.loop(1, 8)
    def _(k):
        came_1(k).wait_recv()

    mine = pl.ds(c * 4, 4)
    other = pl.ds(4 - c * 4, 4)

    def copy_2(k):
        t = at_head(k)
        return remote(rows.at[h, mine], rows.at[h, mine], s2.at[t], r2.at[h], (s, t))

    def came_2(k):
        f = at_head(16 - k)
        return remote(rows.at[f, mine], rows.at[f, mine], s2.at[f], r2.at[f], (s, f))

    def copy_3(k):
        f = at_head(16 - k)
        return remote(rows.at[f, mine], rows.at[f, mine], s3.at[f], r3.at[f], (pair, h))

    def came_3(k):
        f = at_head(16 - k)
        return remote(rows.at[f, other], rows.at[f, other], s3.at[f], r3.at[f], (pair, h))

    @pl.loop(1, 16)
    def _(k):
        copy_2(k).start()

    @pl.loop(0, 16)
    def _(j):
        weight_copy(3, j).wait()

    def block(j, carry):
        acc, squares = carry
        part = rows[j].reshape(128, 512)
        squares = squares + fold_squares(part.astype(F32))
        return acc + jnp.dot(part, wgu[j], preferred_element_type=F32), squares

    carry = block(h, (jnp.zeros((128, 256), F32), jnp.zeros((128, 128), F32)))

    def step(k, carry):
        came_2(k).wait_recv()
        copy_3(k).start()
        came_3(k).wait_recv()
        return block(at_head(16 - k), carry)

    acc, squares = lax.fori_loop(1, 16, step, carry)
    scale = lax.rsqrt(jnp.sum(squares, axis=1, keepdims=True) / D + EPS)
    gate = acc[:, 0:128] * scale
    up = acc[:, 128:256] * scale
    act = (gate / (1.0 + jnp.exp(-gate)) * up).astype(BF)

    def copy_d1(t):
        return remote(send_d1.at[t], recv_d1.at[t], sd1.at[t], rd1.at[t], (pair, h))

    def copy_d2(t):
        return remote(send_d2.at[t], recv_d2.at[h], sd2.at[t], rd2.at[h], (s, t))

    def came_d2(f):
        return remote(send_d2.at[f], recv_d2.at[f], sd2.at[f], rd2.at[f], (s, f))

    @pl.loop(0, 16)
    def _(k):
        t = at_head(k + 1)
        terms = jnp.dot(act, wd[t], preferred_element_type=F32)
        low, high = terms[0:64], terms[64:128]
        own_terms[t] = jnp.where(c == 0, low, high)
        send_d1[t] = jnp.where(c == 0, high, low).astype(BF)
        copy_d1(t).start()

    @pl.loop(0, 15)
    def _(k):
        t = at_head(k + 1)
        copy_d1(t).wait_recv()
        send_d2[t] = (own_terms[t] + recv_d1[t].astype(F32)).astype(BF)
        copy_d2(t).start()

    copy_d1(h).wait_recv()
    own_terms[h] = own_terms[h] + recv_d1[h].astype(F32)

    @pl.loop(1, 16)
    def _(k):
        f = at_head(16 - k)
        came_d2(f).wait_recv()
        own_terms[h] += recv_d2[f].astype(F32)

    def copy_d3(k):
        t = lax.rem(y + k, 4)
        return remote(send_d3.at[t], recv_d3.at[y], sd3.at[t], rd3.at[y], (t * 2 + c, h))

    def came_d3(k):
        f = lax.rem(y + 4 - k, 4)
        return remote(send_d3.at[f], recv_d3.at[f], sd3.at[f], rd3.at[f], (f * 2 + c, h))

    send_d3[...] = own_terms[h].reshape(4, 16, 512).astype(BF)
    for k in range(1, 4):
        copy_d3(k).start()
    total = res[...] + own_terms[h, pl.ds(pl.multiple_of(y * 16, 16), 16)]
    for k in range(1, 4):
        came_d3(k).wait_recv()
        total = total + recv_d3[lax.rem(y + 4 - k, 4)].astype(F32)
    out_ref[...] = total.astype(BF)

    for copy in sends:
        copy.wait_send()

    @pl.loop(1, 16)
    def _(k):
        copy_t(k).wait_send()
        copy_a(k).wait_send()
        copy_2(k).wait_send()
        copy_3(k).wait_send()
        copy_d1(at_head(k)).wait_send()
        copy_d2(at_head(k)).wait_send()

    copy_d1(h).wait_send()

    @pl.loop(1, 8)
    def _(k):
        copy_1(k).wait_send()
        copy_q(k).wait_send()
        copy_p(k).wait_send()

    for k in range(1, 4):
        copy_d3(k).wait_send()


def local(
    hidden_states, span_group, span_slot, span_block, prompt_len, new_tokens, norm_gain, w_q, w_kv, w_o, w_gate_up, w_down
):
    s = lax.axis_index("seq")
    gains = norm_gain.astype(F32)
    freqs = jnp.exp(jnp.arange(HD // 2).astype(F32) * (-2.0 * math.log(THETA) / HD))
    my_group = lax.dynamic_slice_in_dim(span_group[:, 0], s * CD, CD)
    my_slot = lax.dynamic_slice_in_dim(span_slot, s * CD, CD)
    my_block = lax.dynamic_slice_in_dim(span_block, s * CD, CD)
    base = (my_block * C).astype(F32)[:, None] * freqs
    step = jnp.asarray(np.arange(C), F32)[:, None] * freqs
    base_cos, base_sin = jnp.cos(base)[:, None], jnp.sin(base)[:, None]
    step_cos, step_sin = jnp.cos(step)[None], jnp.sin(step)[None]
    cos_k = (base_cos * step_cos - base_sin * step_sin).reshape(CD * C, HD // 2)
    sin_k = (base_sin * step_cos + base_cos * step_sin).reshape(CD * C, HD // 2)
    positions = prompt_len[None, :] + jnp.arange(2, dtype=jnp.int32)[:, None]
    angles = positions.reshape(16).astype(F32)[:, None] * freqs
    cos_q, sin_q = jnp.cos(angles), jnp.sin(angles)
    offsets = (my_block[:, None] * C + jnp.arange(C)).reshape(1, CD * C).astype(F32)
    wanted = (my_group * 32 + my_slot)[None, :] + jnp.arange(4)[:, None] * 8
    sel = (wanted.reshape(32, 1) == jnp.arange(256)[None, :]).astype(BF)
    owner = span_group[:, 0] * 8 + span_slot
    match = (owner[None, :] == (s * 8 + jnp.arange(8))[:, None]).astype(F32)
    lengths = jnp.concatenate([prompt_len // 128, prompt_len % 128]).astype(BF)
    rep_kv = jnp.broadcast_to(gains[0][:, None], (D, 4)).reshape(128, 1, 256)
    rep_gu = jnp.broadcast_to(gains[1][:, None], (D, 2)).reshape(64, 1, 256)
    packed_kv = w_kv.reshape(D, 2, 2, HD).transpose(0, 2, 1, 3).reshape(D * 4, HD)

    vmem = pl.BlockSpec(memory_space=pltpu.VMEM)
    hbm = pl.BlockSpec(memory_space=pl.ANY)
    dma = pltpu.SemaphoreType.DMA
    out = pl.pallas_call(
        layer_kernel,
        name="layer",
        out_shape=jax.ShapeDtypeStruct((16, 512), BF),
        in_specs=[vmem] * 13 + [hbm] * 5,
        out_specs=vmem,
        scratch_shapes=[
            pltpu.VMEM((16, 512, 256), BF),
            pltpu.VMEM((16, 2048, 128), BF),
            pltpu.VMEM((16, 512, 512), BF),
            pltpu.VMEM((16, 256, 512), BF),
            pltpu.VMEM((16, 512, 256), BF),
            pltpu.VMEM((16, 128, 512), BF),
            pltpu.VMEM((256, 256), F32),
            pltpu.VMEM((256, 256), F32),
            pltpu.VMEM((16, 512, 512), BF),
            pltpu.VMEM((512, 512), F32),
            pltpu.VMEM((512, 128), F32),
            pltpu.VMEM((16, 16, 512), BF),
            pltpu.VMEM((8, 32, 256), BF),
            pltpu.VMEM((8, 32, 256), F32),
            pltpu.VMEM((4, 16, 128), F32),
            pltpu.VMEM((16, 16, 512), BF),
            pltpu.VMEM((16, 16, 512), BF),
            pltpu.VMEM((16, 8, 16, 512), BF),
            pltpu.VMEM((16, 64, 512), F32),
            pltpu.VMEM((16, 64, 512), BF),
            pltpu.VMEM((16, 64, 512), BF),
            pltpu.VMEM((16, 64, 512), BF),
            pltpu.VMEM((16, 64, 512), BF),
            pltpu.VMEM((4, 16, 512), BF),
            pltpu.VMEM((4, 16, 512), BF),
            pltpu.VMEM((16, 512), F32),
            dma((4, 16)), dma((16,)), dma((48,)), dma((16, 4)), dma((16,)), dma((16,)), dma((8,)), dma((8,)), dma((8,)), dma((8,)),
            dma((16,)), dma((16,)), dma((8,)), dma((8,)), dma((16,)), dma((16,)), dma((16,)), dma((16,)),
            dma((16,)), dma((16,)), dma((16,)), dma((16,)), dma((4,)), dma((4,)),
        ],
        compiler_params=pltpu.CompilerParams(
            collective_id=1, has_side_effects=True, vmem_limit_bytes=60 * 2**20
        ),
    )(
        hidden_states.reshape(CD * C, 512),
        new_tokens.reshape(16, 512),
        gains[0].reshape(16, 1, 512),
        rep_kv,
        rep_gu,
        sel,
        match,
        offsets,
        jnp.concatenate([cos_k, cos_k], axis=1),
        jnp.concatenate([-sin_k, sin_k], axis=1),
        jnp.concatenate([cos_q, cos_q], axis=1),
        jnp.concatenate([-sin_q, sin_q], axis=1),
        jnp.broadcast_to(lengths[:, None], (16, 256)),
        w_q,
        packed_kv,
        w_o,
        w_gate_up.reshape(D * 2, HD),
        w_down,
    )
    return out.reshape(2, 8, 512)


def solution(mesh):
    placed = (
        P("seq", None, "head"),
        P(),
        P(),
        P(),
        P("seq"),
        P(None, "seq", "head"),
        P(),
        P(None, "head"),
        P(None, None, "head"),
        P("head", None),
        P(None, None, ("seq", "head")),
        P(("seq", "head"), None),
    )
    return jax.shard_map(
        local, mesh=mesh, in_specs=placed, out_specs=P(None, "seq", "head"), check_vma=False
    )
```

```python
import math

import jax
import jax.numpy as jnp
import numpy as np
from jax import lax
from jax.experimental import pallas as pl
from jax.experimental.pallas import tpu as pltpu
from jax.sharding import PartitionSpec as P

D = 8192
HD = 128
C = 64
CD = 8
EPS = 1e-05
THETA = 10000.0
MASKED = -1e30
SCALE = 1.0 / math.sqrt(HD)
MESH = pl.DeviceIdType.MESH
BF = jnp.bfloat16
F32 = jnp.float32


def fold_squares(part, weight):
    sq = part * part * weight
    return (sq[:, 0:128] + sq[:, 128:256]) + (sq[:, 256:384] + sq[:, 384:512])


def rotate(vectors, cosine, sine):
    return vectors * cosine + pltpu.roll(vectors, 64, 1) * sine


ORDER = (
    (-1, 0), (1, 0), (0, -1), (0, 1), (2, 0), (-1, -1), (1, 1), (-1, 1), (1, -1), (0, 2),
    (2, -1), (2, 1), (-1, 2), (1, 2), (2, 2),
)


def layer_kernel(
    x_ref, tok_ref, gain_ref, group_ref, slot_ref, block_ref, length_ref, freq_ref, step_ref, wq_hbm, wkv_hbm, wo_hbm, wgu_hbm, wd_hbm, out_ref,
    wq, raw, raw_gu, wkv, wo, wgu, wd, pick_kv, pick_gu, inv_gain, cosk, sink, cosq, sinq, spans, kv_acc, span_ss, toks, queries, partials, fresh,
    send_a, recv_a, rows, own_terms, send_d1, recv_d1, send_e, recv_e, send_f, recv_f, send_d3, recv_d3, res,
    gu_acc, row_ss,
    wsem, gsem, sx, rx, st, rt, sq, rq, sp, rp,
    sa, ra, s1, r1, s2, r2, s3, r3, sd1, rd1, se, re, sf, rf, sd3, rd3,
):
    s = lax.axis_index("seq")
    h = lax.axis_index("head")
    y = s // 2
    c = lax.rem(s, 2)
    slot = c * 4 + y
    pair = s + 1 - 2 * c
    px = h // 4
    pz = lax.rem(h, 4)

    def at_head(k):
        return lax.rem(h + k, 16)

    def at_seq(k):
        return lax.rem(s + k, 8)

    barrier = pltpu.get_barrier_semaphore()

    @pl.loop(1, 16)
    def _(k):
        pl.semaphore_signal(barrier, inc=1, device_id=(s, at_head(k)), device_id_type=MESH)

    @pl.loop(1, 8)
    def _(k):
        pl.semaphore_signal(barrier, inc=1, device_id=(at_seq(k), h), device_id_type=MESH)

    def weight_copy(which, j):
        cols = pl.ds(pl.multiple_of(j * 512, 512), 512)
        if which == 0:
            return pltpu.make_async_copy(wkv_hbm.at[pl.ds(pl.multiple_of(j * 2048, 2048), 2048)], raw.at[j], wsem.at[0, j])
        if which == 1:
            return pltpu.make_async_copy(wq_hbm.at[cols], wq.at[j], wsem.at[1, j])
        if which == 2:
            return pltpu.make_async_copy(wo_hbm.at[:, cols], wo.at[j], wsem.at[2, j])
        return pltpu.make_async_copy(wd_hbm.at[:, cols], wd.at[j], wsem.at[3, j])

    def gate_up_copy(j):
        return pltpu.make_async_copy(
            wgu_hbm.at[pl.ds(pl.multiple_of(j * 1024, 1024), 1024)], raw_gu.at[j], gsem.at[j]
        )

    for which in range(4):
        @pl.loop(0, 16)
        def _(j):
            weight_copy(which, j).start()

    @pl.loop(0, 16)
    def _(j):
        gate_up_copy(j).start()

    def remote(src, dst, ssem, rsem, device):
        return pltpu.make_async_remote_copy(
            src_ref=src, dst_ref=dst, send_sem=ssem, recv_sem=rsem, device_id=device, device_id_type=MESH
        )

    row = lax.broadcasted_iota(jnp.int32, (256, 256), 0)
    col = lax.broadcasted_iota(jnp.int32, (256, 256), 1)
    low = lax.rem(col, 4)
    pick_kv[...] = jnp.where(row == (lax.rem(low, 2) * 2 + low // 2) * 64 + col // 4, 1.0, 0.0).astype(BF)
    pick_gu[...] = jnp.where(row == lax.rem(col, 2) * 128 + col // 2, 1.0, 0.0).astype(BF)

    own_gain = gain_ref[:, pl.ds(pl.multiple_of(h * 512, 512), 512)].astype(F32)
    spans[h] = (x_ref[...].astype(F32) * own_gain[0:1]).astype(BF)
    toks[h] = (tok_ref[...].astype(F32) * own_gain[0:1]).astype(BF)

    def per_row(shape, values):
        rows_of = lax.rem(lax.broadcasted_iota(jnp.int32, shape, 0), 8)
        out = jnp.zeros(shape, jnp.int32)
        for i, value in enumerate(values):
            out = jnp.where(rows_of == i, value, out)
        return out

    lengths = per_row((8, 256), [length_ref[i] for i in range(8)])
    queries[s, 16:32] = jnp.concatenate([lengths // 128, lax.rem(lengths, 128)], axis=0).astype(F32).astype(BF)
    kv_acc[...] = jnp.zeros_like(kv_acc)
    span_ss[...] = jnp.zeros_like(span_ss)

    pl.semaphore_wait(barrier, 22)

    def make_tables():
        @pl.loop(0, 16)
        def _(j):
            g = gain_ref[:, pl.ds(pl.multiple_of(j * 512, 512), 512)].astype(F32)
            inv_gain[j] = 1.0 / (g * g)

        freq = freq_ref[...]
        sign = jnp.where(lax.broadcasted_iota(jnp.int32, (1, 128), 1) < 64, -1.0, 1.0).astype(F32)
        base = (per_row((8, 128), [block_ref[s * CD + i] for i in range(CD)]) * C).astype(F32) * freq
        base_cos, base_sin = jnp.cos(base), jnp.sin(base)
        step_cos, step_sin = step_ref[0], step_ref[1]
        for i in range(CD):
            bc, bs = base_cos[i:i + 1], base_sin[i:i + 1]
            cosk[i * C:(i + 1) * C] = bc * step_cos - bs * step_sin
            sink[i * C:(i + 1) * C] = (bs * step_cos + bc * step_sin) * sign
        later = lax.broadcasted_iota(jnp.int32, (16, 128), 0) // 8
        at = jnp.concatenate([lengths[:, 0:128], lengths[:, 0:128]], axis=0) + later
        angle = at.astype(F32) * freq
        cosq[...] = jnp.cos(angle)
        sinq[...] = jnp.sin(angle) * sign

    def copy_t(k):
        t = at_head(k)
        return remote(toks.at[h], toks.at[h], st.at[t], rt.at[h], (s, t))

    def came_t(k):
        f = at_head(16 - k)
        return remote(toks.at[f], toks.at[f], st.at[f], rt.at[f], (s, f))

    @pl.loop(1, 16)
    def _(k):
        copy_t(k).start()

    def place(half, a, b):
        dx, dz = (a, b) if half == 0 else (b, a)
        return lax.rem(px + dx + 4, 4) * 4 + lax.rem(pz + dz + 4, 4)

    sends = []

    def push(half, block, part, axis, way):
        there = place(half, way, 0) if axis == 0 else place(half, 0, way)
        first, size, sem = ((0, 128, 0), (128, 128, 1), (0, 256, 0))[part]
        where = spans.at[block, pl.ds(half * 256 + first, size)]
        copy = remote(where, where, sx.at[len(sends)], rx.at[block, half * 2 + sem], (s, there))
        copy.start()
        sends.append(copy)

    def wait_for(half, block, part):
        first, size, sem = ((0, 128, 0), (128, 128, 1), (0, 256, 0))[part]
        where = spans.at[block, pl.ds(half * 256 + first, size)]
        remote(where, where, sx.at[0], rx.at[block, half * 2 + sem], (s, h)).wait_recv()

    def unpack(block):
        weight_copy(0, block).wait()

        @pl.loop(0, 4)
        def _(b):
            part = raw[block, pl.ds(pl.multiple_of(b * 512, 512), 512)]
            part = jnp.concatenate([part[0:256], part[256:512]], axis=1)
            got = jnp.dot(pick_kv[...], part, preferred_element_type=F32).astype(BF)
            for i in range(4):
                for e in range(2):
                    at = pl.ds(pl.multiple_of(b * 128 + e * 64, 64), 64)
                    wkv[block, at, pl.ds(i * 128, 128)] = got[i * 64:(i + 1) * 64, e * 128:(e + 1) * 128]

    def unpack_gate_up(block):
        gate_up_copy(block).wait()

        @pl.loop(0, 2)
        def _(b):
            part = raw_gu[block, pl.ds(pl.multiple_of(b * 512, 512), 512)]
            part = jnp.concatenate([part[0:256], part[256:512]], axis=1)
            got = jnp.dot(pick_gu[...], part, preferred_element_type=F32).astype(BF)
            for i in range(2):
                for e in range(2):
                    at = pl.ds(pl.multiple_of(b * 256 + e * 128, 128), 128)
                    wgu[block, at, pl.ds(i * 128, 128)] = got[i * 128:(i + 1) * 128, e * 128:(e + 1) * 128]

    def take(block):
        @pl.loop(0, 2)
        def _(i):
            at = pl.ds(pl.multiple_of(i * 256, 256), 256)
            part = spans[block, at]
            span_ss[at] += fold_squares(part.astype(F32), inv_gain[block, 0:1])
            kv_acc[at] += jnp.dot(part, wkv[block], preferred_element_type=F32)

    for half in range(2):
        for way in (1, -1):
            push(half, h, 2, 0, way)
    for half in range(2):
        for way in (1, -1):
            push(half, h, 2, 1, way)

    make_tables()
    unpack(h)
    take(h)
    unpack_gate_up(15)

    def project_queries():
        @pl.loop(0, 16)
        def _(j):
            weight_copy(1, j).wait()

        @pl.loop(1, 16)
        def _(k):
            came_t(k).wait_recv()

        def body(j, carry):
            acc, ss = carry
            part = toks[j]
            ss = ss + fold_squares(part.astype(F32), inv_gain[j, 0:1])
            return acc + jnp.dot(part, wq[j], preferred_element_type=F32), ss

        acc, ss = lax.fori_loop(0, 16, body, (jnp.zeros((16, 256), F32), jnp.zeros((16, 128), F32)))
        scale = lax.rsqrt(jnp.sum(ss, axis=1, keepdims=True) / D + EPS)
        for j in range(2):
            at = slice(j * 128, (j + 1) * 128)
            queries[s, 0:16, at] = rotate(acc[:, at] * scale, cosq[...], sinq[...]).astype(BF)

        @pl.loop(1, 8)
        def _(k):
            copy_q(k).start()

        return scale

    def copy_q(k):
        t = at_seq(k)
        return remote(queries.at[s], queries.at[s], sq.at[t], rq.at[s], (t, h))

    def came_q(k):
        f = at_seq(8 - k)
        return remote(queries.at[f], queries.at[f], sq.at[f], rq.at[f], (f, h))

    arrived = [set(), set()]
    taken = {(0, 0)}
    token_scale = None
    for number, (a, b) in enumerate(ORDER):
        ready = sorted((arrived[0] & arrived[1]) - taken)
        for half in range(2):
            block = place(half, a, b)
            parts = (0, 1) if (a == 2 and b == 0) or b == 2 else (2,)
            for part in parts:
                wait_for(half, block, part)
            if b == 0:
                if a == -1:
                    push(half, block, 0, 0, 1)
                if a == 1:
                    push(half, block, 1, 0, -1)
                push(half, block, 2, 1, 1)
                push(half, block, 2, 1, -1)
            elif b == -1:
                push(half, block, 0, 1, 1)
            elif b == 1:
                push(half, block, 1, 1, -1)
            arrived[half].add((a % 4, b % 4) if half == 0 else (b % 4, a % 4))
        for source in ready[:2]:
            taken.add(source)
            unpack(place(0, *source))
            take(place(0, *source))
        unpack_gate_up(number)
        if number == 3:
            token_scale = project_queries()
    for source in sorted((arrived[0] & arrived[1]) - taken):
        unpack(place(0, *source))
        take(place(0, *source))

    lane = lax.broadcasted_iota(jnp.int32, (32, 256), 1)
    line = lax.broadcasted_iota(jnp.int32, (32, 256), 0)
    wanted = per_row((32, 256), [group_ref[s * CD + i] * 32 + slot_ref[s * CD + i] for i in range(CD)]) + line // 8 * 8
    sel = jnp.where(lane == wanted, 1.0, 0.0).astype(BF)
    lane = lax.broadcasted_iota(jnp.int32, (1, 512), 1)
    offset = lax.rem(lane, C)
    position = offset
    for i in range(CD):
        position = jnp.where(lane // C == i, block_ref[s * CD + i] * C + offset, position)
    position = position.astype(F32)
    lane = lax.broadcasted_iota(jnp.int32, (8, 64), 1)
    owner = jnp.zeros((8, 64), jnp.int32)
    for i in range(64):
        owner = jnp.where(lane == i, group_ref[i] * 8 + slot_ref[i], owner)
    match = owner == s * 8 + lax.broadcasted_iota(jnp.int32, (8, 64), 0)

    @pl.loop(1, 8)
    def _(k):
        came_q(k).wait_recv()

    chosen = jnp.dot(sel, queries[...].reshape(256, 256), preferred_element_type=F32)
    length = chosen[16:24, 0:1] * 128.0 + chosen[24:32, 0:1]
    length = jnp.concatenate([length, length], axis=0)
    token_span = lax.broadcasted_iota(jnp.int32, (16, 512), 1) // C
    row_span = lax.rem(lax.broadcasted_iota(jnp.int32, (16, 512), 0), CD)
    live = (token_span == row_span) & (position < length)
    span_scale = lax.rsqrt(jnp.sum(span_ss[...], axis=1, keepdims=True) / D + EPS)
    lanes = lax.broadcasted_iota(jnp.int32, (16, 128), 1)
    for j in range(2):
        at = slice(j * 128, (j + 1) * 128)
        keys = rotate(kv_acc[:, at] * span_scale, cosk[...], sink[...]).astype(BF)
        values = (kv_acc[:, 256 + j * 128:384 + j * 128] * span_scale).astype(BF)
        scores = lax.dot_general(
            chosen[0:16, at].astype(BF), keys, (((1,), (1,)), ((), ())), preferred_element_type=F32
        ) * SCALE
        scores = jnp.where(live, scores, MASKED)
        top = jnp.max(scores, axis=1, keepdims=True)
        weights = jnp.where(live, jnp.exp(scores - top), 0.0)
        total = jnp.sum(weights, axis=1, keepdims=True)
        partials[s, j * 16:(j + 1) * 16, 0:128] = jnp.dot(weights.astype(BF), values, preferred_element_type=F32)
        partials[s, j * 16:(j + 1) * 16, 128:256] = jnp.where(lanes < 64, top, total)

    def copy_p(k):
        t = at_seq(k)
        return remote(partials.at[s], partials.at[s], sp.at[t], rp.at[s], (t, h))

    def came_p(k):
        f = at_seq(8 - k)
        return remote(partials.at[f], partials.at[f], sp.at[f], rp.at[f], (f, h))

    @pl.loop(1, 8)
    def _(k):
        copy_p(k).start()

    def project_fresh(j, acc):
        return acc + jnp.dot(toks[j], wkv[j], preferred_element_type=F32)

    new_kv = lax.fori_loop(0, 16, project_fresh, jnp.zeros((16, 512), F32)) * token_scale
    for j in range(2):
        at = slice(j * 128, (j + 1) * 128)
        fresh[j] = rotate(new_kv[:, at], cosq[...], sinq[...]).astype(BF).astype(F32)
        fresh[2 + j] = new_kv[:, 256 + j * 128:384 + j * 128].astype(BF).astype(F32)

    @pl.loop(1, 8)
    def _(k):
        came_p(k).wait_recv()

    own_q = queries[s, 0:16].astype(F32)
    heads = []
    for j in range(2):
        steps = []
        for t in range(2):
            block = partials[:, pl.ds(j * 16 + t * 8, 8), :].reshape(64, 256)
            stats = block[:, 128:256].T
            tops, sums = stats[0:8], stats[64:72]
            q = own_q[t * 8:(t + 1) * 8, j * 128:(j + 1) * 128]
            fresh_scores = [
                jnp.sum(q * fresh[j, u * 8:(u + 1) * 8], axis=1, keepdims=True) * SCALE for u in range(t + 1)
            ]
            best = jnp.max(jnp.where(match, tops, MASKED), axis=1, keepdims=True)
            for score in fresh_scores:
                best = jnp.maximum(best, score)
            factor = jnp.where(match, jnp.exp(jnp.where(match, tops, best) - best), 0.0)
            total = jnp.sum(factor * sums, axis=1, keepdims=True)
            value = jnp.dot(factor, block[:, 0:128], precision=lax.Precision.HIGHEST, preferred_element_type=F32)
            for u, score in enumerate(fresh_scores):
                e = jnp.exp(score - best)
                total = total + e
                value = value + e * fresh[2 + j, u * 8:(u + 1) * 8]
            steps.append(value / total)
        heads.append(jnp.concatenate(steps, axis=0))
    att = jnp.concatenate(heads, axis=1).astype(BF)

    @pl.loop(0, 16)
    def _(j):
        weight_copy(2, j).wait()

    def copy_a(k):
        t = at_head(k)
        return remote(send_a.at[t], recv_a.at[h], sa.at[t], ra.at[h], (s, t))

    def came_a(k):
        f = at_head(16 - k)
        return remote(send_a.at[f], recv_a.at[f], sa.at[f], ra.at[f], (s, f))

    @pl.loop(1, 16)
    def _(k):
        t = at_head(k)
        send_a[t] = jnp.dot(att, wo[t], preferred_element_type=F32).astype(BF)
        copy_a(k).start()

    res[...] = tok_ref[...].astype(F32) + jnp.dot(att, wo[h], preferred_element_type=F32)

    @pl.loop(1, 16)
    def _(k):
        came_a(k).wait_recv()
        res[...] += recv_a[at_head(16 - k)].astype(F32)

    rows[h, slot] = (res[...] * own_gain[1:2]).astype(BF)

    def copy_1(k):
        t = lax.rem(s + k, 8)
        return remote(rows.at[h, slot], rows.at[h, slot], s1.at[t], r1.at[s], (t, h))

    def came_1(k):
        f = lax.rem(s + 8 - k, 8)
        place = lax.rem(f, 2) * 4 + f // 2
        return remote(rows.at[h, place], rows.at[h, place], s1.at[f], r1.at[f], (f, h))

    @pl.loop(1, 8)
    def _(k):
        copy_1(k).start()

    @pl.loop(1, 8)
    def _(k):
        came_1(k).wait_recv()

    def rows_of(block, core, half):
        return rows.at[block, pl.ds(core * 4 + half * 2, 2)]

    row_sends = []

    def spread(half, block, axis, way):
        there = place(half, way, 0) if axis == 0 else place(half, 0, way)
        where = rows_of(block, c, half)
        copy = remote(where, where, s2.at[len(row_sends)], r2.at[block, half], (s, there))
        copy.start()
        row_sends.append(copy)

    def to_pair(half, block):
        where = rows_of(block, c, half)
        return remote(where, where, s3.at[block, half], r3.at[block, half], (pair, h))

    def came(half, block):
        where = rows_of(block, c, half)
        remote(where, where, s2.at[0], r2.at[block, half], (s, h)).wait_recv()
        to_pair(half, block).start()

    for axis in range(2):
        for way in range(1, 4):
            for half in range(2):
                spread(half, h, axis, way)

    @pl.loop(0, 16)
    def _(j):
        weight_copy(3, j).wait()

    gu_acc[...] = jnp.zeros_like(gu_acc)
    row_ss[...] = jnp.zeros_like(row_ss)

    def use_rows(block):
        part = rows[block].reshape(128, 512)
        row_ss[...] += fold_squares(part.astype(F32), inv_gain[block, 1:2])
        gu_acc[...] += jnp.dot(part, wgu[block], preferred_element_type=F32)

    use_rows(h)
    for a in range(1, 4):
        for half in range(2):
            block = place(half, a, 0)
            came(half, block)
            for way in range(1, 4):
                spread(half, block, 1, way)
    done = {(0, 0)}
    for a in range(4):
        for b in range(1, 4):
            for half in range(2):
                came(half, place(half, a, b))
        for source in [(i, j) for i in range(a + 1 if a else 4) for j in range(a + 1 if a else 4)]:
            if source in done or (a == 0 and 0 not in source):
                continue
            done.add(source)
            block = place(0, *source)
            for half in range(2):
                where = rows_of(block, 1 - c, half)
                remote(where, where, s3.at[block, half], r3.at[block, half], (pair, h)).wait_recv()
            use_rows(block)

    acc = gu_acc[...]
    squares = row_ss[...]
    scale = lax.rsqrt(jnp.sum(squares, axis=1, keepdims=True) / D + EPS)
    gate = acc[:, 0:128] * scale
    up = acc[:, 128:256] * scale
    act = (gate / (1.0 + jnp.exp(-gate)) * up).astype(BF)

    def copy_d1(t):
        return remote(send_d1.at[t], recv_d1.at[t], sd1.at[t], rd1.at[t], (pair, h))

    here = (px, pz)

    def copy_e(half, k):
        mine = here[half]
        t = lax.rem(mine + k, 4)
        f = lax.rem(mine + 4 - k, 4)
        return (
            remote(send_e.at[half, t], recv_e.at[half, mine], se.at[half, t], re.at[half, mine], (s, place(half, k, 0))),
            remote(send_e.at[half, f], recv_e.at[half, f], se.at[half, f], re.at[half, f], (s, h)),
            f,
        )

    def copy_f(half, k):
        mine = here[1 - half]
        t = lax.rem(mine + k, 4)
        f = lax.rem(mine + 4 - k, 4)
        return (
            remote(send_f.at[half, t], recv_f.at[half, mine], sf.at[half, t], rf.at[half, mine], (s, place(half, 0, k))),
            remote(send_f.at[half, f], recv_f.at[half, f], sf.at[half, f], rf.at[half, f], (s, h)),
            f,
        )

    line = [(a, b) for a in (1, 2, 3, 0) for b in (1, 2, 3, 0)]
    for a, b in line:
        t = place(0, a, b)
        terms = jnp.dot(act, wd[t], preferred_element_type=F32)
        first, last = terms[0:64], terms[64:128]
        own_terms[t] = jnp.where(c == 0, first, last)
        send_d1[t] = jnp.where(c == 0, last, first).astype(BF)
        copy_d1(t).start()

    for a, b in line:
        t = place(0, a, b)
        tx, tz = lax.rem(px + a, 4), lax.rem(pz + b, 4)
        copy_d1(t).wait_recv()
        total = own_terms[t] + recv_d1[t].astype(F32)
        if a:
            send_e[0, tx, tz] = total[0:32].astype(BF)
        else:
            own_terms[t, 0:32] = total[0:32]
        if b:
            send_e[1, tz, tx] = total[32:64].astype(BF)
        else:
            own_terms[t, 32:64] = total[32:64]
        if a and b == 0:
            copy_e(0, a)[0].start()
        if a == 0 and b:
            copy_e(1, b)[0].start()

    for k in range(1, 4):
        for half in range(2):
            _, came_e, f = copy_e(half, k)
            came_e.wait_recv()
            for i in range(4):
                t = place(half, 0, i)
                at = slice(half * 32, half * 32 + 32)
                own_terms[t, at] += recv_e[half, f, lax.rem(here[1 - half] + i, 4)].astype(F32)

    for k in range(1, 4):
        for half in range(2):
            t = place(half, 0, k)
            send_f[half, lax.rem(here[1 - half] + k, 4)] = own_terms[t, half * 32:half * 32 + 32].astype(BF)
            copy_f(half, k)[0].start()

    for k in range(1, 4):
        for half in range(2):
            _, came_f, f = copy_f(half, k)
            came_f.wait_recv()
            own_terms[h, half * 32:half * 32 + 32] += recv_f[half, f].astype(F32)

    def copy_d3(k):
        t = lax.rem(y + k, 4)
        return remote(send_d3.at[t], recv_d3.at[y], sd3.at[t], rd3.at[y], (t * 2 + c, h))

    def came_d3(k):
        f = lax.rem(y + 4 - k, 4)
        return remote(send_d3.at[f], recv_d3.at[f], sd3.at[f], rd3.at[f], (f * 2 + c, h))

    send_d3[...] = own_terms[h].reshape(4, 16, 512).astype(BF)
    for k in range(1, 4):
        copy_d3(k).start()
    total = res[...] + own_terms[h, pl.ds(pl.multiple_of(y * 16, 16), 16)]
    for k in range(1, 4):
        came_d3(k).wait_recv()
        total = total + recv_d3[lax.rem(y + 4 - k, 4)].astype(F32)
    out_ref[...] = total.astype(BF)

    for copy in sends + row_sends:
        copy.wait_send()

    for k in range(1, 4):
        for half in range(2):
            copy_e(half, k)[0].wait_send()
            copy_f(half, k)[0].wait_send()

    @pl.loop(1, 16)
    def _(k):
        copy_t(k).wait_send()
        copy_a(k).wait_send()
        for half in range(2):
            to_pair(half, at_head(k)).wait_send()
        copy_d1(at_head(k)).wait_send()

    copy_d1(h).wait_send()

    @pl.loop(1, 8)
    def _(k):
        copy_1(k).wait_send()
        copy_q(k).wait_send()
        copy_p(k).wait_send()

    for k in range(1, 4):
        copy_d3(k).wait_send()


def local(
    hidden_states, span_group, span_slot, span_block, prompt_len, new_tokens, norm_gain, w_q, w_kv, w_o, w_gate_up, w_down
):
    freqs = np.tile(THETA ** (-np.arange(HD // 2) * 2.0 / HD), 2)[None, :]
    steps = np.arange(C)[:, None] * freqs
    packed_kv = w_kv.reshape(D, 2, 2, HD).transpose(0, 2, 1, 3).reshape(D * 4, HD)

    vmem = pl.BlockSpec(memory_space=pltpu.VMEM)
    smem = pl.BlockSpec(memory_space=pltpu.SMEM)
    hbm = pl.BlockSpec(memory_space=pl.ANY)
    dma = pltpu.SemaphoreType.DMA
    out = pl.pallas_call(
        layer_kernel,
        name="layer",
        out_shape=jax.ShapeDtypeStruct((16, 512), BF),
        in_specs=[vmem] * 3 + [smem] * 4 + [vmem] * 2 + [hbm] * 5,
        out_specs=vmem,
        scratch_shapes=[
            pltpu.VMEM((16, 512, 256), BF),
            pltpu.VMEM((16, 2048, 128), BF),
            pltpu.VMEM((16, 1024, 128), BF),
            pltpu.VMEM((16, 512, 512), BF),
            pltpu.VMEM((16, 256, 512), BF),
            pltpu.VMEM((16, 512, 256), BF),
            pltpu.VMEM((16, 128, 512), BF),
            pltpu.VMEM((256, 256), BF),
            pltpu.VMEM((256, 256), BF),
            pltpu.VMEM((16, 2, 512), F32),
            pltpu.VMEM((512, 128), F32),
            pltpu.VMEM((512, 128), F32),
            pltpu.VMEM((16, 128), F32),
            pltpu.VMEM((16, 128), F32),
            pltpu.VMEM((16, 512, 512), BF),
            pltpu.VMEM((512, 512), F32),
            pltpu.VMEM((512, 128), F32),
            pltpu.VMEM((16, 16, 512), BF),
            pltpu.VMEM((8, 32, 256), BF),
            pltpu.VMEM((8, 32, 256), F32),
            pltpu.VMEM((4, 16, 128), F32),
            pltpu.VMEM((16, 16, 512), BF),
            pltpu.VMEM((16, 16, 512), BF),
            pltpu.VMEM((16, 8, 16, 512), BF),
            pltpu.VMEM((16, 64, 512), F32),
            pltpu.VMEM((16, 64, 512), BF),
            pltpu.VMEM((16, 64, 512), BF),
            pltpu.VMEM((2, 4, 4, 32, 512), BF),
            pltpu.VMEM((2, 4, 4, 32, 512), BF),
            pltpu.VMEM((2, 4, 32, 512), BF),
            pltpu.VMEM((2, 4, 32, 512), BF),
            pltpu.VMEM((4, 16, 512), BF),
            pltpu.VMEM((4, 16, 512), BF),
            pltpu.VMEM((16, 512), F32),
            pltpu.VMEM((128, 256), F32),
            pltpu.VMEM((128, 128), F32),
            dma((4, 16)), dma((16,)), dma((48,)), dma((16, 4)), dma((16,)), dma((16,)), dma((8,)), dma((8,)), dma((8,)), dma((8,)),
            dma((16,)), dma((16,)), dma((8,)), dma((8,)), dma((32,)), dma((16, 2)), dma((16, 2)), dma((16, 2)),
            dma((16,)), dma((16,)), dma((2, 4)), dma((2, 4)), dma((2, 4)), dma((2, 4)), dma((4,)), dma((4,)),
        ],
        compiler_params=pltpu.CompilerParams(
            collective_id=1, has_side_effects=True, vmem_limit_bytes=60 * 2**20
        ),
    )(
        hidden_states.reshape(CD * C, 512),
        new_tokens.reshape(16, 512),
        norm_gain,
        span_group.reshape(64),
        span_slot,
        span_block,
        prompt_len,
        jnp.asarray(freqs, F32),
        jnp.asarray(np.stack([np.cos(steps), np.sin(steps)]), F32),
        w_q,
        packed_kv,
        w_o,
        w_gate_up.reshape(D * 2, HD),
        w_down,
    )
    return out.reshape(2, 8, 512)


def solution(mesh):
    placed = (
        P("seq", None, "head"),
        P(),
        P(),
        P(),
        P("seq"),
        P(None, "seq", "head"),
        P(),
        P(None, "head"),
        P(None, None, "head"),
        P("head", None),
        P(None, None, ("seq", "head")),
        P(("seq", "head"), None),
    )
    return jax.shard_map(
        local, mesh=mesh, in_specs=placed, out_specs=P(None, "seq", "head"), check_vma=False
    )
```

```python
import math

import jax
import jax.numpy as jnp
import numpy as np
from jax import lax
from jax.experimental import pallas as pl
from jax.experimental.pallas import tpu as pltpu
from jax.sharding import PartitionSpec as P

D = 8192
HD = 128
C = 64
CD = 8
EPS = 1e-05
THETA = 10000.0
MASKED = -1e30
SCALE = 1.0 / math.sqrt(HD)
MESH = pl.DeviceIdType.MESH
BF = jnp.bfloat16
F32 = jnp.float32


def fold_squares(part, weight):
    sq = part * part * weight
    return (sq[:, 0:128] + sq[:, 128:256]) + (sq[:, 256:384] + sq[:, 384:512])


def rotate(vectors, cosine, sine):
    return vectors * cosine + pltpu.roll(vectors, 64, 1) * sine


ORDER = (
    (-1, 0), (0, -1), (0, 1), (1, 0), (0, 2), (-1, -1), (-1, 1), (2, 0), (1, -1), (1, 1),
    (-1, 2), (2, -1), (2, 1), (1, 2), (2, 2),
)


def layer_kernel(
    x_ref, tok_ref, gain_ref, group_ref, slot_ref, block_ref, length_ref, freq_ref, step_ref, wq_hbm, wkv_hbm, wo_hbm, wgu_hbm, wd_hbm, out_ref,
    wq, raw, raw_gu, wkv, wo, wgu, wd, pick_kv, pick_gu, inv_gain, cosk, sink, cosq, sinq, spans, kv_acc, span_ss, toks, queries, partials, fresh,
    send_a, recv_a, rows, own_terms, send_d1, recv_d1, send_e, recv_e, send_g, recv_g, res,
    gu_acc, row_ss,
    wsem, gsem, sx, rx, st, rt, sq, rq, sp, rp,
    sa, ra, s1, r1, s2, r2, s3, r3, sd1, rd1, se, re, sg, rg,
):
    s = lax.axis_index("seq")
    h = lax.axis_index("head")
    y = s // 2
    c = lax.rem(s, 2)
    slot = c * 4 + y
    pair = s + 1 - 2 * c
    px = h // 4
    pz = lax.rem(h, 4)

    def at_head(k):
        return lax.rem(h + k, 16)

    def at_seq(k):
        return lax.rem(s + k, 8)

    def place(half, a, b):
        dx, dz = (a, b) if half == 0 else (b, a)
        return lax.rem(px + dx + 4, 4) * 4 + lax.rem(pz + dz + 4, 4)

    barrier = pltpu.get_barrier_semaphore()

    @pl.loop(1, 16)
    def _(k):
        pl.semaphore_signal(barrier, inc=1, device_id=(s, at_head(k)), device_id_type=MESH)

    @pl.loop(1, 8)
    def _(k):
        pl.semaphore_signal(barrier, inc=1, device_id=(at_seq(k), h), device_id_type=MESH)

    def at_y(k):
        return lax.rem(y + k, 4) * 2 + c

    for half in range(2):
        @pl.loop(1, 4)
        def _(i):
            @pl.loop(1, 4)
            def _(k):
                pl.semaphore_signal(barrier, inc=1, device_id=(at_y(i), place(half, k, 0)), device_id_type=MESH)

    def kv_copy(j):
        return pltpu.make_async_copy(wkv_hbm.at[pl.ds(pl.multiple_of(j * 2048, 2048), 2048)], raw.at[j], gsem.at[j])

    wq_copy = pltpu.make_async_copy(wq_hbm, wq, wsem.at[0])
    gu_copy = pltpu.make_async_copy(wgu_hbm, raw_gu, wsem.at[1])
    wo_copy = pltpu.make_async_copy(wo_hbm, wo, wsem.at[2])
    wd_copy = pltpu.make_async_copy(wd_hbm, wd, wsem.at[3])

    def block_at(j):
        return pl.ds(pl.multiple_of(j * 512, 512), 512)

    def remote(src, dst, ssem, rsem, device):
        return pltpu.make_async_remote_copy(
            src_ref=src, dst_ref=dst, send_sem=ssem, recv_sem=rsem, device_id=device, device_id_type=MESH
        )

    own_gain = gain_ref[:, pl.ds(pl.multiple_of(h * 512, 512), 512)].astype(F32)
    spans[h] = (x_ref[...].astype(F32) * own_gain[0:1]).astype(BF)
    toks[h] = (tok_ref[...].astype(F32) * own_gain[0:1]).astype(BF)

    def per_row(shape, values):
        rows_of = lax.rem(lax.broadcasted_iota(jnp.int32, shape, 0), 8)
        out = jnp.zeros(shape, jnp.int32)
        for i, value in enumerate(values):
            out = jnp.where(rows_of == i, value, out)
        return out

    lengths = per_row((8, 256), [length_ref[i] for i in range(8)])
    queries[s, 16:32] = jnp.concatenate([lengths // 128, lax.rem(lengths, 128)], axis=0).astype(F32).astype(BF)
    pl.semaphore_wait(barrier, 40)

    def make_tables():
        @pl.loop(0, 16)
        def _(j):
            g = gain_ref[:, pl.ds(pl.multiple_of(j * 512, 512), 512)].astype(F32)
            inv_gain[j] = 1.0 / (g * g)

        freq = freq_ref[...]
        sign = jnp.where(lax.broadcasted_iota(jnp.int32, (1, 128), 1) < 64, -1.0, 1.0).astype(F32)
        base = (per_row((8, 128), [block_ref[s * CD + i] for i in range(CD)]) * C).astype(F32) * freq
        base_cos, base_sin = jnp.cos(base), jnp.sin(base)
        step_cos, step_sin = step_ref[0], step_ref[1]
        for i in range(CD):
            bc, bs = base_cos[i:i + 1], base_sin[i:i + 1]
            cosk[i * C:(i + 1) * C] = bc * step_cos - bs * step_sin
            sink[i * C:(i + 1) * C] = (bs * step_cos + bc * step_sin) * sign
        later = lax.broadcasted_iota(jnp.int32, (16, 128), 0) // 8
        at = jnp.concatenate([lengths[:, 0:128], lengths[:, 0:128]], axis=0) + later
        angle = at.astype(F32) * freq
        cosq[...] = jnp.cos(angle)
        sinq[...] = jnp.sin(angle) * sign

    def copy_t(k):
        t = at_head(k)
        return remote(toks.at[h], toks.at[h], st.at[t], rt.at[h], (s, t))

    def came_t(k):
        f = at_head(16 - k)
        return remote(toks.at[f], toks.at[f], st.at[f], rt.at[f], (s, f))

    sends = []

    def push(half, block, part, axis, way):
        there = place(half, way, 0) if axis == 0 else place(half, 0, way)
        first, size, sem = ((0, 128, 0), (128, 128, 1), (0, 256, 0))[part]
        where = spans.at[block, pl.ds(half * 256 + first, size)]
        copy = remote(where, where, sx.at[len(sends)], rx.at[block, half * 2 + sem], (s, there))
        copy.start()
        sends.append(copy)

    def wait_for(half, block, part):
        first, size, sem = ((0, 128, 0), (128, 128, 1), (0, 256, 0))[part]
        where = spans.at[block, pl.ds(half * 256 + first, size)]
        remote(where, where, sx.at[0], rx.at[block, half * 2 + sem], (s, h)).wait_recv()

    def unpack(block):
        kv_copy(block).wait()

        @pl.loop(0, 4)
        def _(b):
            part = raw[block, pl.ds(pl.multiple_of(b * 512, 512), 512)]
            part = jnp.concatenate([part[0:256], part[256:512]], axis=1)
            got = jnp.dot(pick_kv[...], part, preferred_element_type=F32).astype(BF)
            for i in range(4):
                for e in range(2):
                    at = pl.ds(pl.multiple_of(b * 128 + e * 64, 64), 64)
                    wkv[block, at, pl.ds(i * 128, 128)] = got[i * 64:(i + 1) * 64, e * 128:(e + 1) * 128]

    def unpack_gate_up(block):
        @pl.loop(0, 2)
        def _(b):
            part = raw_gu[pl.ds(pl.multiple_of(block * 1024 + b * 512, 512), 512)]
            part = jnp.concatenate([part[0:256], part[256:512]], axis=1)
            got = jnp.dot(pick_gu[...], part, preferred_element_type=F32).astype(BF)
            for i in range(2):
                for e in range(2):
                    at = pl.ds(pl.multiple_of(b * 256 + e * 128, 128), 128)
                    wgu[block, at, pl.ds(i * 128, 128)] = got[i * 128:(i + 1) * 128, e * 128:(e + 1) * 128]

    def take(block):
        @pl.loop(0, 2)
        def _(i):
            at = pl.ds(pl.multiple_of(i * 256, 256), 256)
            part = spans[block, at]
            span_ss[at] += fold_squares(part.astype(F32), inv_gain[block, 0:1])
            kv_acc[at] += jnp.dot(part, wkv[block], preferred_element_type=F32)

    for half in range(2):
        for way in (1, -1):
            push(half, h, 2, 0, way)
    for half in range(2):
        for way in (1, -1):
            push(half, h, 2, 1, way)

    @pl.loop(1, 16)
    def _(k):
        copy_t(k).start()

    @pl.loop(0, 16)
    def _(j):
        kv_copy(at_head(j)).start()

    for copy in (wq_copy, gu_copy, wo_copy, wd_copy):
        copy.start()

    row = lax.broadcasted_iota(jnp.int32, (256, 256), 0)
    col = lax.broadcasted_iota(jnp.int32, (256, 256), 1)
    low = lax.rem(col, 4)
    pick_kv[...] = jnp.where(row == (lax.rem(low, 2) * 2 + low // 2) * 64 + col // 4, 1.0, 0.0).astype(BF)
    pick_gu[...] = jnp.where(row == lax.rem(col, 2) * 128 + col // 2, 1.0, 0.0).astype(BF)

    kv_acc[...] = jnp.zeros_like(kv_acc)
    span_ss[...] = jnp.zeros_like(span_ss)
    make_tables()
    unpack(h)
    take(h)

    def project_queries():
        wq_copy.wait()

        @pl.loop(1, 16)
        def _(k):
            came_t(k).wait_recv()

        def body(j, carry):
            acc, ss = carry
            part = toks[j]
            ss = ss + fold_squares(part.astype(F32), inv_gain[j, 0:1])
            return acc + jnp.dot(part, wq[block_at(j)], preferred_element_type=F32), ss

        acc, ss = lax.fori_loop(0, 16, body, (jnp.zeros((16, 256), F32), jnp.zeros((16, 128), F32)))
        scale = lax.rsqrt(jnp.sum(ss, axis=1, keepdims=True) / D + EPS)
        for j in range(2):
            at = slice(j * 128, (j + 1) * 128)
            queries[s, 0:16, at] = rotate(acc[:, at] * scale, cosq[...], sinq[...]).astype(BF)

        @pl.loop(1, 8)
        def _(k):
            copy_q(k).start()

        return scale

    def copy_q(k):
        t = at_seq(k)
        return remote(queries.at[s], queries.at[s], sq.at[t], rq.at[s], (t, h))

    def came_q(k):
        f = at_seq(8 - k)
        return remote(queries.at[f], queries.at[f], sq.at[f], rq.at[f], (f, h))

    arrived = [set(), set()]
    unpacked = {(0, 0)}
    taken = {(0, 0)}
    upcoming = []
    for a, b in ORDER:
        for source in ((a % 4, b % 4), (b % 4, a % 4)):
            if source not in upcoming:
                upcoming.append(source)

    def unpack_once(source):
        if source not in unpacked:
            unpacked.add(source)
            unpack(place(0, *source))

    def take_ready(most):
        for source in [u for u in upcoming if u in arrived[0] and u in arrived[1] and u not in taken][:most]:
            taken.add(source)
            unpack_once(source)
            take(place(0, *source))

    token_scale = None
    for number, (a, b) in enumerate(ORDER):
        if b == 2:
            take_ready(15)
            for source in [u for u in upcoming if u not in unpacked][:3]:
                unpack_once(source)
        had = sum(u in arrived[0] and u in arrived[1] and u not in taken for u in upcoming)
        for half in range(2):
            block = place(half, a, b)
            parts = (0, 1) if (a == 2 and b == 0) or b == 2 else (2,)
            for part in parts:
                wait_for(half, block, part)
            if b == 0:
                if a == -1:
                    push(half, block, 0, 0, 1)
                if a == 1:
                    push(half, block, 1, 0, -1)
                push(half, block, 2, 1, 1)
                push(half, block, 2, 1, -1)
            elif b == -1:
                push(half, block, 0, 1, 1)
            elif b == 1:
                push(half, block, 1, 1, -1)
        if b != 2:
            take_ready(min(had, 2))
        for half in range(2):
            arrived[half].add((a % 4, b % 4) if half == 0 else (b % 4, a % 4))
        if 6 <= number <= 13:
            if number == 6:
                gu_copy.wait()
            unpack_gate_up(2 * number - 12)
            unpack_gate_up(2 * number - 11)
        if number == 3:
            token_scale = project_queries()
    take_ready(15)

    lane = lax.broadcasted_iota(jnp.int32, (32, 256), 1)
    line = lax.broadcasted_iota(jnp.int32, (32, 256), 0)
    wanted = per_row((32, 256), [group_ref[s * CD + i] * 32 + slot_ref[s * CD + i] for i in range(CD)]) + line // 8 * 8
    sel = jnp.where(lane == wanted, 1.0, 0.0).astype(BF)
    lane = lax.broadcasted_iota(jnp.int32, (1, 512), 1)
    offset = lax.rem(lane, C)
    position = offset
    for i in range(CD):
        position = jnp.where(lane // C == i, block_ref[s * CD + i] * C + offset, position)
    position = position.astype(F32)
    lane = lax.broadcasted_iota(jnp.int32, (8, 64), 1)
    owner = jnp.zeros((8, 64), jnp.int32)
    for i in range(64):
        owner = jnp.where(lane == i, group_ref[i] * 8 + slot_ref[i], owner)
    match = owner == s * 8 + lax.broadcasted_iota(jnp.int32, (8, 64), 0)

    @pl.loop(1, 8)
    def _(k):
        came_q(k).wait_recv()

    chosen = jnp.dot(sel, queries[...].reshape(256, 256), preferred_element_type=F32)
    length = chosen[16:24, 0:1] * 128.0 + chosen[24:32, 0:1]
    length = jnp.concatenate([length, length], axis=0)
    token_span = lax.broadcasted_iota(jnp.int32, (16, 512), 1) // C
    row_span = lax.rem(lax.broadcasted_iota(jnp.int32, (16, 512), 0), CD)
    live = (token_span == row_span) & (position < length)
    span_scale = lax.rsqrt(jnp.sum(span_ss[...], axis=1, keepdims=True) / D + EPS)
    lanes = lax.broadcasted_iota(jnp.int32, (16, 128), 1)
    for j in range(2):
        at = slice(j * 128, (j + 1) * 128)
        keys = rotate(kv_acc[:, at] * span_scale, cosk[...], sink[...]).astype(BF)
        values = (kv_acc[:, 256 + j * 128:384 + j * 128] * span_scale).astype(BF)
        scores = lax.dot_general(
            chosen[0:16, at].astype(BF), keys, (((1,), (1,)), ((), ())), preferred_element_type=F32
        ) * SCALE
        scores = jnp.where(live, scores, MASKED)
        top = jnp.max(scores, axis=1, keepdims=True)
        weights = jnp.where(live, jnp.exp(scores - top), 0.0)
        total = jnp.sum(weights, axis=1, keepdims=True)
        summed = jnp.dot(weights.astype(BF), values, preferred_element_type=F32)
        partials[s, j * 16:(j + 1) * 16, 0:128] = summed.astype(BF)
        top_high = top.astype(BF).astype(F32)
        top_mid = (top - top_high).astype(BF).astype(F32)
        total_high = total.astype(BF).astype(F32)
        stats = jnp.where(lanes < 16, top_high, top_mid)
        stats = jnp.where(lanes < 32, stats, top - top_high - top_mid)
        stats = jnp.where(lanes < 48, stats, total_high)
        stats = jnp.where(lanes < 64, stats, total - total_high)
        partials[s, j * 16:(j + 1) * 16, 128:256] = stats.astype(BF)

    def copy_p(k):
        t = at_seq(k)
        return remote(partials.at[s], partials.at[s], sp.at[t], rp.at[s], (t, h))

    def came_p(k):
        f = at_seq(8 - k)
        return remote(partials.at[f], partials.at[f], sp.at[f], rp.at[f], (f, h))

    @pl.loop(1, 8)
    def _(k):
        copy_p(k).start()

    def project_fresh(j, acc):
        return acc + jnp.dot(toks[j], wkv[j], preferred_element_type=F32)

    new_kv = lax.fori_loop(0, 16, project_fresh, jnp.zeros((16, 512), F32)) * token_scale
    for j in range(2):
        at = slice(j * 128, (j + 1) * 128)
        fresh[j] = rotate(new_kv[:, at], cosq[...], sinq[...]).astype(BF).astype(F32)
        fresh[2 + j] = new_kv[:, 256 + j * 128:384 + j * 128].astype(BF).astype(F32)

    @pl.loop(1, 8)
    def _(k):
        came_p(k).wait_recv()

    own_q = queries[s, 0:16].astype(F32)
    arrived_parts = [[partials[i:i + 1, j * 16:(j + 1) * 16].astype(F32) for i in range(8)] for j in range(2)]
    heads = []
    for j in range(2):
        steps = []
        for t in range(2):
            block = jnp.concatenate([both[:, t * 8:(t + 1) * 8] for both in arrived_parts[j]], axis=0).reshape(64, 256)
            stats = block[:, 128:256].T
            tops, sums = stats[0:8] + stats[16:24] + stats[32:40], stats[48:56] + stats[64:72]
            q = own_q[t * 8:(t + 1) * 8, j * 128:(j + 1) * 128]
            fresh_scores = [
                jnp.sum(q * fresh[j, u * 8:(u + 1) * 8], axis=1, keepdims=True) * SCALE for u in range(t + 1)
            ]
            best = jnp.max(jnp.where(match, tops, MASKED), axis=1, keepdims=True)
            for score in fresh_scores:
                best = jnp.maximum(best, score)
            factor = jnp.where(match, jnp.exp(jnp.where(match, tops, best) - best), 0.0)
            total = jnp.sum(factor * sums, axis=1, keepdims=True)
            value = jnp.dot(factor, block[:, 0:128], precision=lax.Precision.HIGHEST, preferred_element_type=F32)
            for u, score in enumerate(fresh_scores):
                e = jnp.exp(score - best)
                total = total + e
                value = value + e * fresh[2 + j, u * 8:(u + 1) * 8]
            steps.append(value / total)
        heads.append(jnp.concatenate(steps, axis=0))
    att = jnp.concatenate(heads, axis=1).astype(BF)

    wo_copy.wait()

    def copy_a(k):
        t = at_head(k)
        return remote(send_a.at[t], recv_a.at[h], sa.at[t], ra.at[h], (s, t))

    def came_a(k):
        f = at_head(16 - k)
        return remote(send_a.at[f], recv_a.at[f], sa.at[f], ra.at[f], (s, f))

    for first in range(1, 16, 5):
        for k in range(first, first + 5):
            t = at_head(k)
            send_a[t] = jnp.dot(att, wo[:, block_at(t)], preferred_element_type=F32).astype(BF)
        for k in range(first, first + 5):
            copy_a(k).start()

    summed = tok_ref[...].astype(F32) + jnp.dot(att, wo[:, block_at(h)], preferred_element_type=F32)
    for k in range(1, 16):
        came_a(k).wait_recv()
        summed = summed + recv_a[at_head(16 - k)].astype(F32)
    res[...] = summed

    rows[h, slot] = (res[...] * own_gain[1:2]).astype(BF)
    own_half = y // 2
    own_line = jnp.where(own_half == 0, px, pz)

    def copy_1(i, k):
        there = jnp.where(own_half == 0, place(0, k, 0), place(1, k, 0))
        where = rows.at[h, slot]
        return remote(where, where, s1.at[i, k], r1.at[own_half, lax.rem(y, 2), own_line], (at_y(i), there))

    for i in range(4):
        for k in range(4):
            if i or k:
                copy_1(i, k).start()

    def came_1(half, i, k):
        where = rows.at[place(half, k, 0), c * 4 + half * 2 + i]
        line = lax.rem((px, pz)[half] + k, 4)
        remote(where, where, s1.at[0, 1], r1.at[half, i, line], (s, h)).wait_recv()

    def rows_of(block, core, half):
        return rows.at[block, pl.ds(core * 4 + half * 2, 2)]

    row_sends = []

    def spread(half, block, axis, way):
        there = place(half, way, 0) if axis == 0 else place(half, 0, way)
        where = rows_of(block, c, half)
        copy = remote(where, where, s2.at[len(row_sends)], r2.at[block, half], (s, there))
        copy.start()
        row_sends.append(copy)

    def to_pair(half, block):
        where = rows_of(block, c, half)
        return remote(where, where, s3.at[block, half], r3.at[block, half], (pair, h))

    def came(half, block):
        where = rows_of(block, c, half)
        remote(where, where, s2.at[0], r2.at[block, half], (s, h)).wait_recv()
        to_pair(half, block).start()

    wd_copy.wait()

    gu_acc[...] = jnp.zeros_like(gu_acc)
    row_ss[...] = jnp.zeros_like(row_ss)

    def use_rows(block):
        part = rows[block].reshape(128, 512)
        row_ss[...] += fold_squares(part.astype(F32), inv_gain[block, 1:2])
        gu_acc[...] += jnp.dot(part, wgu[block], preferred_element_type=F32)

    for k in range(4):
        for half in range(2):
            block = place(half, k, 0)
            for i in range(2):
                if k:
                    came_1(half, i, k)
                else:
                    @pl.when(y != half * 2 + i)
                    def _():
                        came_1(half, i, k)
            for way in range(1, 4):
                spread(half, block, 1, way)
            to_pair(half, block).start()
    have = [{(k, 0) for k in range(4)}, {(0, k) for k in range(4)}]
    used = set()

    def use_ready(ready):
        for source in ready:
            used.add(source)
            block = place(0, *source)
            for half in range(2):
                where = rows_of(block, 1 - c, half)
                remote(where, where, s3.at[block, half], r3.at[block, half], (pair, h)).wait_recv()
            use_rows(block)

    for a in range(4):
        for b in range(1, 4):
            ready = sorted((have[0] & have[1]) - used)
            for half in range(2):
                came(half, place(half, a, b))
                have[half].add((a, b) if half == 0 else (b, a))
            use_ready(ready)
    use_ready(sorted((have[0] & have[1]) - used))

    acc = gu_acc[...]
    squares = row_ss[...]
    scale = lax.rsqrt(jnp.sum(squares, axis=1, keepdims=True) / D + EPS)
    gate = acc[:, 0:128] * scale
    up = acc[:, 128:256] * scale
    act = (gate / (1.0 + jnp.exp(-gate)) * up).astype(BF)

    def copy_d1(t):
        return remote(send_d1.at[t], recv_d1.at[t], sd1.at[t], rd1.at[t], (pair, h))

    here = (px, pz)

    def copy_e(half, k):
        mine = here[half]
        t = lax.rem(mine + k, 4)
        f = lax.rem(mine + 4 - k, 4)
        return (
            remote(send_e.at[half, t], recv_e.at[half, mine], se.at[half, t], re.at[half, mine], (s, place(half, k, 0))),
            remote(send_e.at[half, f], recv_e.at[half, f], se.at[half, f], re.at[half, f], (s, h)),
            f,
        )

    def copy_g(half, i, k):
        return remote(
            send_g.at[half, i, k], recv_g.at[here[1 - half], y], sg.at[half, i, k], rg.at[here[1 - half], y],
            ((half * 2 + i) * 2 + c, place(half, 0, k)),
        )

    def each_g(do):
        for k in (1, 2, 3, 0):
            for half in range(2):
                for i in range(2):
                    if k:
                        do(copy_g(half, i, k))
                    else:
                        @pl.when(y != half * 2 + i)
                        def _():
                            do(copy_g(half, i, k))

    def make_terms(a, b):
        t = place(0, a, b)
        terms = jnp.dot(act, wd[:, block_at(t)], preferred_element_type=F32)
        first, last = terms[0:64], terms[64:128]
        own_terms[t] = jnp.where(c == 0, first, last)
        send_d1[t] = jnp.where(c == 0, last, first).astype(BF)
        copy_d1(t).start()

    passed = set()

    def pass_terms(a, b):
        t = place(0, a, b)
        tx, tz = lax.rem(px + a, 4), lax.rem(pz + b, 4)
        copy_d1(t).wait_recv()
        total = own_terms[t] + recv_d1[t].astype(F32)
        if a:
            send_e[0, tx, tz] = total[0:32].astype(BF)
        else:
            own_terms[t, 0:32] = total[0:32]
        if b:
            send_e[1, tz, tx] = total[32:64].astype(BF)
        else:
            own_terms[t, 32:64] = total[32:64]
        passed.add((a, b))
        if a and {(a, k) for k in range(4)} <= passed:
            copy_e(0, a)[0].start()
        if b and {(k, b) for k in range(4)} <= passed:
            copy_e(1, b)[0].start()

    line = [
        (1, 1), (1, 2), (1, 3), (1, 0), (2, 1), (3, 1), (0, 1), (2, 2), (2, 3), (2, 0), (3, 2), (0, 2), (3, 3), (3, 0), (0, 3), (0, 0),
    ]
    lag = 3
    for number in range(16 + lag):
        if number < 16:
            make_terms(*line[number])
        if number >= lag:
            pass_terms(*line[number - lag])

    for k in range(1, 4):
        for half in range(2):
            _, came_e, f = copy_e(half, k)
            came_e.wait_recv()
            for i in range(4):
                t = place(half, 0, i)
                at = slice(half * 32, half * 32 + 32)
                own_terms[t, at] += recv_e[half, f, lax.rem(here[1 - half] + i, 4)].astype(F32)

    for k in range(4):
        for half in range(2):
            for i in range(2):
                at = half * 32 + i * 16
                send_g[half, i, k] = own_terms[place(half, 0, k), at:at + 16].astype(BF)
    each_g(lambda copy: copy.start())

    total = res[...] + own_terms[h, pl.ds(pl.multiple_of(y * 16, 16), 16)]
    last_line = jnp.where(own_half == 0, pz, px)
    for i in range(4):
        for k in range(4):
            if i or k:
                line, f = lax.rem(last_line + k, 4), lax.rem(y + i, 4)
                remote(send_g.at[0, 0, 1], recv_g.at[line, f], sg.at[0, 0, 1], rg.at[line, f], (s, h)).wait_recv()
                total = total + recv_g[line, f].astype(F32)
    out_ref[...] = total.astype(BF)

    for copy in sends + row_sends:
        copy.wait_send()

    for k in range(1, 4):
        for half in range(2):
            copy_e(half, k)[0].wait_send()

    @pl.loop(1, 16)
    def _(k):
        copy_t(k).wait_send()
        copy_a(k).wait_send()
        for half in range(2):
            to_pair(half, at_head(k)).wait_send()
        copy_d1(at_head(k)).wait_send()

    copy_d1(h).wait_send()

    for half in range(2):
        to_pair(half, h).wait_send()
    each_g(lambda copy: copy.wait_send())
    for i in range(4):
        for k in range(4):
            if i or k:
                copy_1(i, k).wait_send()

    @pl.loop(1, 8)
    def _(k):
        copy_q(k).wait_send()
        copy_p(k).wait_send()


def local(
    hidden_states, span_group, span_slot, span_block, prompt_len, new_tokens, norm_gain, w_q, w_kv, w_o, w_gate_up, w_down
):
    freqs = np.tile(THETA ** (-np.arange(HD // 2) * 2.0 / HD), 2)[None, :]
    steps = np.arange(C)[:, None] * freqs
    packed_kv = w_kv.reshape(D, 2, 2, HD).transpose(0, 2, 1, 3).reshape(D * 4, HD)

    vmem = pl.BlockSpec(memory_space=pltpu.VMEM)
    smem = pl.BlockSpec(memory_space=pltpu.SMEM)
    hbm = pl.BlockSpec(memory_space=pl.ANY)
    dma = pltpu.SemaphoreType.DMA
    out = pl.pallas_call(
        layer_kernel,
        name="layer",
        out_shape=jax.ShapeDtypeStruct((16, 512), BF),
        in_specs=[vmem] * 3 + [smem] * 4 + [vmem] * 2 + [hbm] * 5,
        out_specs=vmem,
        scratch_shapes=[
            pltpu.VMEM((D, 256), BF),
            pltpu.VMEM((16, 2048, 128), BF),
            pltpu.VMEM((2 * D, 128), BF),
            pltpu.VMEM((16, 512, 512), BF),
            pltpu.VMEM((256, D), BF),
            pltpu.VMEM((16, 512, 256), BF),
            pltpu.VMEM((128, D), BF),
            pltpu.VMEM((256, 256), BF),
            pltpu.VMEM((256, 256), BF),
            pltpu.VMEM((16, 2, 512), F32),
            pltpu.VMEM((512, 128), F32),
            pltpu.VMEM((512, 128), F32),
            pltpu.VMEM((16, 128), F32),
            pltpu.VMEM((16, 128), F32),
            pltpu.VMEM((16, 512, 512), BF),
            pltpu.VMEM((512, 512), F32),
            pltpu.VMEM((512, 128), F32),
            pltpu.VMEM((16, 16, 512), BF),
            pltpu.VMEM((8, 32, 256), BF),
            pltpu.VMEM((8, 32, 256), BF),
            pltpu.VMEM((4, 16, 128), F32),
            pltpu.VMEM((16, 16, 512), BF),
            pltpu.VMEM((16, 16, 512), BF),
            pltpu.VMEM((16, 8, 16, 512), BF),
            pltpu.VMEM((16, 64, 512), F32),
            pltpu.VMEM((16, 64, 512), BF),
            pltpu.VMEM((16, 64, 512), BF),
            pltpu.VMEM((2, 4, 4, 32, 512), BF),
            pltpu.VMEM((2, 4, 4, 32, 512), BF),
            pltpu.VMEM((2, 2, 4, 16, 512), BF),
            pltpu.VMEM((4, 4, 16, 512), BF),
            pltpu.VMEM((16, 512), F32),
            pltpu.VMEM((128, 256), F32),
            pltpu.VMEM((128, 128), F32),
            dma((4,)), dma((16,)), dma((48,)), dma((16, 4)), dma((16,)), dma((16,)), dma((8,)), dma((8,)), dma((8,)), dma((8,)),
            dma((16,)), dma((16,)), dma((4, 4)), dma((2, 2, 4)), dma((32,)), dma((16, 2)), dma((16, 2)), dma((16, 2)),
            dma((16,)), dma((16,)), dma((2, 4)), dma((2, 4)), dma((2, 2, 4)), dma((4, 4)),
        ],
        compiler_params=pltpu.CompilerParams(
            collective_id=1, has_side_effects=True, vmem_limit_bytes=60 * 2**20
        ),
    )(
        hidden_states.reshape(CD * C, 512),
        new_tokens.reshape(16, 512),
        norm_gain,
        span_group.reshape(64),
        span_slot,
        span_block,
        prompt_len,
        jnp.asarray(freqs, F32),
        jnp.asarray(np.stack([np.cos(steps), np.sin(steps)]), F32),
        w_q,
        packed_kv,
        w_o,
        w_gate_up.reshape(D * 2, HD),
        w_down,
    )
    return out.reshape(2, 8, 512)


def solution(mesh):
    placed = (
        P("seq", None, "head"),
        P(),
        P(),
        P(),
        P("seq"),
        P(None, "seq", "head"),
        P(),
        P(None, "head"),
        P(None, None, "head"),
        P("head", None),
        P(None, None, ("seq", "head")),
        P(("seq", "head"), None),
    )
    return jax.shard_map(
        local, mesh=mesh, in_specs=placed, out_specs=P(None, "seq", "head"), check_vma=False
    )
```
